128 devices in a mesh: ep: 16 (over y, x), wide: 8 (over z, core).
Axes of the slice: x: 4, y: 4, z: 4, core: 2. Of those that a mesh axis runs over, the one named last changes fastest.
Arguments:
- requests: bfloat16 [2, 1024, 7168], P(None, ('ep', 'wide')), may hold values from -6 to 6
- routes: int32 [2, 1024, 2], P(None, ('ep', 'wide')), may hold values from 0 to 15, all different within a row
- gates: bfloat16 [2, 1024, 2], P(None, ('ep', 'wide')), may hold values from 0.099609375 to 1
- replica: int32 [1024, 2], P(('ep', 'wide')), may hold values from 0 to 3
- placement: int32 [16], replicated, may hold values from 0 to 15, each once
- copy_plan: int32 [4], replicated, may hold values from 0 to 15, as said below
- capacity: int32 [2, 16], replicated, may hold values from 8 to 16, as said below
- gate_proj: bfloat16 [16, 7168, 2048], P('ep', None, 'wide'), may hold values from -0.0625 to 0.0625
- up_proj: bfloat16 [16, 7168, 2048], P('ep', None, 'wide'), may hold values from -0.0625 to 0.0625
- down_proj: bfloat16 [16, 2048, 7168], P('ep', 'wide'), may hold values from -0.125 to 0.125
Outputs:
- moe_out: bfloat16 [2, 1024, 7168], P(None, ('ep', 'wide'))
The draws below stay inside these ranges and needn't reach their ends.
Inputs may be any that keep to these rules, and one draw needn't show every extreme that they name: `copy_plan`: entries 1 to 3 are the distances 1, half of 16 and 15, in some order. `capacity`: no more than 16, which some device reaches in each step. `routes`: each row names 2 different experts.
All inputs are finite; a program needn't handle non-finite values.
Results may differ from the reference program's by a relative error of at most 0.02.
Values may be sent and summed in bfloat16 or wider, within the bound.
A program may use at most 128 MiB of HBM per device.

```python
import math
import jax
import jax.numpy as jnp
from jax import lax

D = 7168
HID = 2048
STEPS = 2
TOP = 2
CAP = 16
REPL = 3
EXPERTS = 16
HID_DEV = 256
GROUP = 64
ROWS = 1024
N_EP = 16
N_WIDE = 8


def draw_copy_plan(key, part):
    key = jax.random.fold_in(key, 23)
    key_hot, key_order = jax.random.split(key, 2)
    hot = jax.random.randint(key_hot, (1,), 0, EXPERTS)
    distances = jnp.array([1, EXPERTS // 2, EXPERTS - 1], jnp.int32)
    distances = jax.random.permutation(key_order, distances)
    return jnp.concatenate([hot.astype(jnp.int32), distances.astype(jnp.int32)]).astype(jnp.int32)


def draw_capacity(key, part):
    key = jax.random.fold_in(key, 11)
    key_values, key_places = jax.random.split(key)
    values = jax.random.randint(key_values, (STEPS, EXPERTS), CAP // 2, CAP + 1)
    places = jax.random.randint(key_places, (STEPS, 1), 0, EXPERTS)
    columns = jnp.arange(EXPERTS)[None, :]
    return jnp.where(columns == places, CAP, values).astype(jnp.int32)


def plant(values, rng, least, largest):
    longest = values.shape.index(max(values.shape))
    spots = []
    for shift in (0, 1):
        where = [jax.random.randint(jax.random.fold_in(rng, axis), (), 0, length) for axis, length in enumerate(values.shape)]
        where[longest] = (where[longest] + shift) % values.shape[longest]
        spots.append(tuple(where))
    return values.at[spots[0]].set(least).at[spots[1]].set(largest)


def block_scale(key, shape, shards, least, high):
    gain, own = 1.0, jax.random.fold_in(key, 6)
    for dim, shards_of in shards:
        steps = jnp.exp(jax.random.uniform(jax.random.fold_in(own, dim), (shards_of,), jnp.float32, least / len(shards), high / len(shards)))
        gain = gain * jnp.repeat(steps, shape[dim] // shards_of).reshape([-1 if axis == dim else 1 for axis in range(len(shape))])
    return gain


def choose_distinct(stream_key, rows, amount, top, lift):
    ranking = jax.random.permutation(jax.random.fold_in(stream_key, 1), amount)
    favour = ranking
    for power in range(3):
        favour = favour * favour // amount
    favour = favour * lift // amount
    chance = jax.random.randint(jax.random.fold_in(stream_key, 2), (rows, amount), 0, 4096) + favour
    fixed_rows = jax.random.permutation(jax.random.fold_in(stream_key, 3), rows)[jnp.arange(amount) % rows]
    chance = jnp.where(jnp.arange(rows)[:, None] == fixed_rows[None, :], 1 << 14, chance)
    priority = chance * amount + jnp.arange(amount)
    return lax.top_k(priority.astype(jnp.int32), top)[1].astype(jnp.int32)


def normal_values(key, shape, deviation, most, pieces=(), kind=jnp.bfloat16):
    values = jax.random.normal(key, shape, jnp.float32) * deviation
    if len(pieces) > 0:
        values = block_scale(key, shape, pieces, -0.22, 0.18) * values
    return jnp.clip(values, min=-most, max=most).astype(kind)


def setup_inputs(seed: int = 0) -> dict:
    key_list = jax.random.split(jax.random.key(seed), 11)
    requests = normal_values(key_list[0], (STEPS, ROWS, D), 1.0, 6.0, ((1, 128),))
    routes = choose_distinct(key_list[1], STEPS * ROWS, EXPERTS, TOP, 2048).reshape((STEPS, ROWS, TOP))
    gates = jnp.clip(jnp.exp(math.log(1.0) - 2.306499 * jax.random.uniform(key_list[2], (STEPS, ROWS, TOP), jnp.float32) ** block_scale(key_list[2], (STEPS, ROWS, TOP), ((1, 128),), -0.2, 0.2)), 0.099609375, 1.0).astype(jnp.bfloat16)
    replica = plant(jax.random.randint(key_list[3], (ROWS, TOP), 0, REPL + 1), jax.random.fold_in(key_list[3], 1), 0, REPL).astype(jnp.int32)
    placement = jax.random.permutation(key_list[4], EXPERTS).astype(jnp.int32)
    copy_plan = draw_copy_plan(jax.random.fold_in(key_list[10], 71), 0)
    capacity = draw_capacity(jax.random.fold_in(key_list[10], 71), 0)
    gate_proj = normal_values(key_list[7], (EXPERTS, D, HID), D ** -0.5, 0.0625, ((0, 16), (2, 8)))
    up_proj = normal_values(key_list[8], (EXPERTS, D, HID), D ** -0.5, 0.0625, ((0, 16), (2, 8)))
    down_proj = normal_values(key_list[9], (EXPERTS, HID, D), HID ** -0.5, 0.125, ((0, 16), (1, 8)))
    return dict(requests=requests, routes=routes, gates=gates, replica=replica, placement=placement, copy_plan=copy_plan, capacity=capacity, gate_proj=gate_proj, up_proj=up_proj, down_proj=down_proj)


def plan_group(ids, chooser, placement, hot_expert, new_owners, limits, second, experts, slot_count):
    slots = jnp.arange(experts, dtype=jnp.int32)
    server = jnp.sum(jnp.where(ids[..., None] == slots, placement, 0), -1, dtype=jnp.int32)
    copied = jnp.zeros(ids.shape, jnp.int32)
    if second:
        hot = hot_expert[0]
        hot_home = jnp.sum(jnp.where(slots == hot, placement, 0), dtype=jnp.int32)
        candidates = jnp.concatenate([hot_home[None], new_owners]).astype(jnp.int32)
        listed = jnp.arange(candidates.shape[0], dtype=jnp.int32)
        chosen = jnp.sum(jnp.where(chooser[..., None] == listed, candidates, 0), -1, dtype=jnp.int32)
        is_hot = ids == hot
        server = jnp.where(is_hot, chosen, server)
        copied = (is_hot & (chooser > 0)).astype(jnp.int32)
    server = server.reshape(-1)
    copied = copied.reshape(-1)
    onehot = (server[:, None] == slots).astype(jnp.int32)
    before = jnp.cumsum(onehot, 0, dtype=jnp.int32) - onehot
    position = jnp.sum(before * onehot, -1, dtype=jnp.int32)
    limit = jnp.sum(onehot * limits, -1, dtype=jnp.int32)
    kept = (position < limit).astype(jnp.int32)
    places = jnp.arange(slot_count, dtype=jnp.int32)
    match = kept[:, None, None] * onehot[:, :, None] * (position[:, None, None] == places).astype(jnp.int32)
    return match, copied


def expert_rows(rows, gate_w, up_w, down_w):
    gate = jnp.dot(rows, gate_w, preferred_element_type=jnp.float32)
    upper = jnp.dot(rows, up_w, preferred_element_type=jnp.float32)
    hidden = (jax.nn.silu(gate) * upper).astype(jnp.bfloat16)
    count = rows.shape[0]
    blocks = hidden.reshape(count, N_WIDE, HID_DEV).astype(jnp.float32)
    downs = down_w.reshape(N_WIDE, HID_DEV, D).astype(jnp.float32)
    partial_value = jnp.einsum("nwh,whd->nwd", blocks, downs)
    partial_value = lax.optimization_barrier(partial_value.astype(jnp.bfloat16)).astype(jnp.float32)
    return jnp.sum(partial_value, axis=1).astype(jnp.bfloat16)


def reference(requests, routes, gates, replica, placement, copy_plan, capacity, gate_proj, up_proj, down_proj):
    slots = jnp.arange(EXPERTS, dtype=jnp.int32)
    hot_expert = copy_plan[:1].astype(jnp.int32)
    hot_slot = jnp.sum(jnp.where(slots == hot_expert[0], placement, 0), dtype=jnp.int32)
    new_owners = ((hot_slot + copy_plan[1:]) % EXPERTS).astype(jnp.int32)
    chooser = replica.reshape(N_EP, GROUP, TOP)
    results = []
    for step_index in range(STEPS):
        second = step_index == 1
        ids = routes[step_index].reshape(N_EP, GROUP, TOP)
        limits = capacity[step_index]

        def plan_one(group_ids, group_chooser):
            return plan_group(group_ids, group_chooser, placement, hot_expert, new_owners, limits, second, EXPERTS, CAP)

        match, copied = jax.vmap(plan_one)(ids, chooser)
        match_float = match.astype(jnp.float32)
        weights_g = gates[step_index].reshape(N_EP, GROUP * TOP).astype(jnp.float32)
        rows = requests[step_index].reshape(N_EP, GROUP, D).astype(jnp.float32)

        def contribution(selection, server, weight_slot):
            chosen = lax.dynamic_index_in_dim(match_float, server, 2, keepdims=False) * selection[:, :, None]
            dispatch = chosen.reshape(N_EP, GROUP, TOP, CAP).sum(2)
            inputs = jnp.einsum("gsc,gsd->gcd", dispatch, rows, precision=lax.Precision.HIGHEST).astype(jnp.bfloat16)
            served = expert_rows(inputs.reshape(-1, D), gate_proj[weight_slot], up_proj[weight_slot], down_proj[weight_slot])
            served = served.reshape(N_EP, CAP, D).astype(jnp.float32)
            combine = (chosen * weights_g[:, :, None]).reshape(N_EP, GROUP, TOP, CAP).sum(2)
            return jnp.einsum("gsc,gcd->gsd", combine, served, precision=lax.Precision.HIGHEST)

        home_sel = (1 - copied).astype(jnp.float32)
        copy_sel = copied.astype(jnp.float32)

        def home_pass(total, server):
            return total + contribution(home_sel, server, server), None

        total, ignored = lax.scan(home_pass, jnp.zeros((N_EP, GROUP, D), jnp.float32), slots)
        if second:
            def copy_pass(running, owner):
                return running + contribution(copy_sel, owner, hot_slot), None

            total, ignored = lax.scan(copy_pass, total, new_owners)
        results.append(total.reshape(-1, D).astype(jnp.bfloat16))
    return jnp.stack(results)
```

```python
import functools

import jax
import jax.numpy as jnp
import numpy as np
from jax import lax
from jax.experimental import pallas as pl
from jax.experimental.pallas import tpu as pltpu
from jax.sharding import PartitionSpec as P

BF = jnp.bfloat16
F32 = jnp.float32
STEPS = 2
CAP = 16
NE = 16
NW = 8
GROUP = 64
D = 7168
COLS = D // NW
SLOTS = NE * CAP
HALF = SLOTS // 2
HID = 256

STEP_XY = ((1, 0), (-1, 0), (0, 1), (0, -1))
TREES = (
    ((0, 0, 0), (1, 0, 2), (1, 0, 0), (1, 1, 2), (2, 0, 0), (2, 0, 3), (1, 2, 1), (2, 3, 0)),
    ((0, 0, 1), (3, 0, 1), (3, 0, 3), (2, 0, 2), (2, 0, 1), (3, 3, 3), (2, 1, 1), (3, 2, 0)),
    ((0, 0, 2), (0, 1, 1), (0, 1, 0), (0, 1, 2), (3, 1, 3), (1, 1, 3), (3, 1, 2), (3, 2, 2)),
    ((0, 0, 3), (0, 3, 3), (0, 3, 1), (0, 3, 0), (0, 2, 0), (3, 3, 2), (1, 3, 2), (1, 2, 3)),
)
LAG = 2
CHUNKS = 42
T_SLOTS = CHUNKS + 3 * LAG
STAGE = 3


def relay_tables():
    flags = np.zeros((16, 4, 4), np.float32)
    arrive = np.zeros((16, 8), np.int32)
    for tree, edges in enumerate(TREES):
        came = {(0, 0): (None, 0)}
        for x, y, link in edges:
            via, depth = came[(x, y)]
            to = ((x + STEP_XY[link][0]) % 4, (y + STEP_XY[link][1]) % 4)
            assert to not in came
            came[to] = (link, depth + 1)
            place = y * 4 + x
            column = link ^ 1 if via is None else via
            assert flags[place, link].sum() == 0 and (via is None or via != link ^ 1)
            flags[place, link, column] = 1
            arrive[to[1] * 4 + to[0], 2 * tree] = link
            arrive[to[1] * 4 + to[0], 2 * tree + 1] = LAG * depth
    return flags.reshape(16, 16), arrive


FLAGS, ARRIVE = relay_tables()


def rcopy(src, dst, ssem, rsem, dev):
    return pltpu.make_async_remote_copy(
        src_ref=src,
        dst_ref=dst,
        send_sem=ssem,
        recv_sem=rsem,
        device_id=dev,
        device_id_type=pl.DeviceIdType.MESH,
    )


def lanes(start, size):
    return pl.ds(pl.multiple_of(start, 128), size)


def rows16(start, size):
    return pl.ds(pl.multiple_of(start, 16), size)


def layer_kernel(
    req, meta, par, flag, tab, gate, up, down, out,
    xin, xmeta, outg, tgo, tgi, rows, hw, rb, sb, mk, acc, hid, part, sibr, zs, za, zb, rp, rm,
    eo, ret, wc, outb, fin,
    load_sem, x_ss, x_rs, m_ss, m_rs, a_ss, a_rs, t_ss, t_rs, own_sem,
    b_ss, b_rs, gz_ss, gz_rs, gs_ss, gs_rs, s_ss, s_rs, z_ss, z_rs, r_ss, r_rs, f_ss, f_rs,
):
    e = lax.axis_index("ep")
    w = lax.axis_index("wide")
    ex, ey = e % 4, e // 4
    z, c = w // 2, w % 2

    def wide_dev(other):
        return {"ep": e, "wide": other}

    def ep_dev(other):
        return {"ep": other, "wide": w}

    def z_dev(shift):
        return wide_dev(((z + shift) % 4) * 2 + c)

    sibling = wide_dev(z * 2 + 1 - c)
    link_dev = [
        ep_dev(((ey + dy + 4) % 4) * 4 + (ex + dx + 4) % 4) for dx, dy in STEP_XY
    ]

    loads = [
        pltpu.make_async_copy(gate, hw.at[pl.ds(0, 56)], load_sem.at[0]),
        pltpu.make_async_copy(up, hw.at[pl.ds(56, 56)], load_sem.at[1]),
    ]
    for load in loads:
        load.start()

    def load_down(j, carry):
        for half in range(2):
            pltpu.make_async_copy(
                down.at[pl.ds(half * 128, 128), lanes(j * 256, 256)],
                hw.at[112 + 2 * j + half],
                load_sem.at[2],
            ).start()
        return carry

    lax.fori_loop(0, 28, load_down, 0)

    barrier = pltpu.get_barrier_semaphore()
    for j in range(1, NW):
        pl.semaphore_signal(barrier, inc=1, device_id=wide_dev((w + j) % NW), device_id_type=pl.DeviceIdType.MESH)
    for j in range(1, NE):
        pl.semaphore_signal(barrier, inc=1, device_id=ep_dev((e + j) % NE), device_id_type=pl.DeviceIdType.MESH)
    pl.semaphore_wait(barrier, NW - 1 + NE - 1)

    def exchange(j):
        peer = (w + j) % NW
        frm = (w + NW - j) % NW
        return (
            rcopy(req.at[:, lanes(peer * COLS, COLS)], xin.at[w], x_ss.at[j - 1], x_rs.at[j - 1], wide_dev(peer)),
            rcopy(meta, xmeta.at[w], m_ss.at[j - 1], m_rs.at[j - 1], wide_dev(peer)),
            rcopy(req.at[:, lanes(peer * COLS, COLS)], xin.at[frm], x_ss.at[j - 1], x_rs.at[j - 1], wide_dev(peer)),
            rcopy(meta, xmeta.at[frm], m_ss.at[j - 1], m_rs.at[j - 1], wide_dev(peer)),
        )

    for j in range(1, NW):
        copies = exchange(j)
        copies[1].start()
        copies[0].start()
    xin[w] = req[:, lanes(w * COLS, COLS)]
    xmeta[w] = meta[...]

    for link in range(4):
        for k in range(4):
            mk[link * 4 + k] = jnp.full((16, 256), flag[link * 4 + k], F32).astype(BF)

    for load in loads:
        load.wait()
    pltpu.make_async_copy(hw.at[pl.ds(112, 56)], hw.at[pl.ds(112, 56)], load_sem.at[2]).wait()

    def slot_copy(link, t):
        return rcopy(sb.at[link, t % STAGE], rb.at[link, t], b_ss.at[link, t % STAGE], b_rs.at[link, t], link_dev[link])

    def slot(t, with_own, with_recv, with_wait):
        if with_recv:
            for link in range(4):
                slot_copy(link, t - LAG).wait_recv()
        for link in range(4):
            if with_wait:
                slot_copy(link, t - STAGE).wait_send()
            total = None
            for k in range(4):
                if k == link ^ 1:
                    if not with_own:
                        continue
                    block = hw[link * CHUNKS + t]
                else:
                    if not with_recv:
                        continue
                    block = rb[k, t - LAG]
                term = block.reshape(8, 16, 256) * mk[link * 4 + k][None]
                total = term if total is None else total + term
            sb[link, t % STAGE] = total.reshape(128, 256)
            slot_copy(link, t).start()

    cursor = [0]

    def run_slots(count):
        t0 = cursor[0]
        t1 = min(T_SLOTS, t0 + count)
        cursor[0] = t1
        cuts = sorted({t0, t1, *[x for x in (LAG, STAGE, CHUNKS) if t0 < x < t1]})
        for lo, hi in zip(cuts[:-1], cuts[1:]):
            kind = (lo < CHUNKS, lo >= LAG, lo >= STAGE)
            if hi - lo == 1:
                slot(lo, *kind)
            else:
                def body(t, carry, kind=kind):
                    slot(t, *kind)
                    return carry

                lax.fori_loop(lo, hi, body, 0)

    def finish_slots():
        run_slots(T_SLOTS)

        def drain_recv(t, carry):
            for link in range(4):
                slot_copy(link, t).wait_recv()
            return carry

        def drain_send(t, carry):
            for link in range(4):
                slot_copy(link, t).wait_send()
            return carry

        lax.fori_loop(T_SLOTS - LAG, T_SLOTS, drain_recv, 0)
        lax.fori_loop(T_SLOTS - STAGE, T_SLOTS, drain_send, 0)

    def make_plan():
        picks = xmeta[...].reshape(128, 128)
        lane = lax.broadcasted_iota(jnp.int32, (128, 128), 1)
        line = lax.broadcasted_iota(jnp.int32, (128, 128), 0)
        lane_f = lane.astype(F32)
        second = (line // 8) % 2 == 1
        limits = jnp.where(second, jnp.broadcast_to(par[3:4, :], (128, 128)), jnp.broadcast_to(par[2:3, :], (128, 128)))
        place = jnp.broadcast_to(par[0:1, :], (128, 128))
        cand = jnp.broadcast_to(par[1:2, :], (128, 128))
        hot = jnp.broadcast_to(par[4:5, :], (128, 128))
        zero = jnp.zeros((128, 128), F32)

        def spread(column):
            return jnp.broadcast_to(picks[:, column : column + 1], (128, 128))

        def total(v):
            return jnp.broadcast_to(jnp.sum(v, axis=1, keepdims=True), (128, 128))

        onehots, servers, copied = [], [], []
        for k in range(2):
            route, pick = spread(k), spread(2 + k)
            server = total(jnp.where(lane_f == route, place, zero))
            chosen = total(jnp.where(lane_f == pick, cand, zero))
            is_hot = jnp.where(second, jnp.where(route == hot, 1.0, 0.0), 0.0)
            server = jnp.where(is_hot > 0.5, chosen, server)
            copied.append(jnp.where(pick > 0.5, is_hot, 0.0))
            servers.append(server)
            onehots.append(jnp.where(lane_f == server, 1.0, 0.0))
        earlier = jnp.where(lane < line, 1.0, 0.0) * jnp.where((line // 8) % 2 == (lane // 8) % 2, 1.0, 0.0)
        before = jnp.dot(earlier.astype(BF), (onehots[0] + onehots[1]).astype(BF), preferred_element_type=F32)
        lane_w = lax.broadcasted_iota(jnp.int32, (128, 512), 1).astype(F32)
        base = jnp.where(second, float(SLOTS), 0.0)
        matches = []
        for k in range(2):
            count = before if k == 0 else before + onehots[0]
            position = total(count * onehots[k])
            limit = total(limits * onehots[k])
            column = jnp.where(position < limit, base + servers[k] * CAP + position, -1.0)
            matches.append(jnp.where(lane_w == jnp.broadcast_to(column[:, :1], (128, 512)), 1.0, 0.0))

        def wide512(v):
            return jnp.broadcast_to(v[:, :1], (128, 512))

        wc[...] = (matches[0] * wide512(spread(4)) + matches[1] * wide512(spread(5))).astype(BF)
        dispatch = (matches[0] + matches[1]).astype(BF)
        tags = (matches[0] * wide512(copied[0]) + matches[1] * wide512(copied[1])).astype(BF)
        flat = xin[...].reshape(128, COLS)
        contract = (((0,), (0,)), ((), ()))
        for s in range(STEPS):
            outg[s] = lax.dot_general(
                dispatch[:, s * SLOTS : (s + 1) * SLOTS], flat, contract, preferred_element_type=F32
            ).astype(BF)
        tgo[...] = lax.dot_general(
            tags[:, SLOTS:], jnp.ones((128, 128), BF), contract, preferred_element_type=F32
        ).astype(BF)

    def a2a_start(s):
        def send(j, carry):
            peer = (e + j) % NE
            rcopy(
                outg.at[s, rows16(peer * CAP, CAP)], rows.at[s, rows16(e * CAP, CAP), lanes(w * COLS, COLS)],
                a_ss.at[s], a_rs.at[s], ep_dev(peer),
            ).start()
            if s == 1:
                rcopy(
                    tgo.at[rows16(peer * CAP, CAP)], tgi.at[rows16(e * CAP, CAP)], t_ss, t_rs, ep_dev(peer)
                ).start()
            return carry

        lax.fori_loop(1, NE, send, 0)
        rows[s, rows16(e * CAP, CAP), lanes(w * COLS, COLS)] = outg[s, rows16(e * CAP, CAP), :]
        if s == 1:
            tgi[rows16(e * CAP, CAP), :] = tgo[rows16(e * CAP, CAP), :]

    def a2a_wait(s):
        n = (NE - 1) * CAP
        done = rcopy(
            outg.at[s, pl.ds(0, n)], rows.at[s, pl.ds(0, n), lanes(w * COLS, COLS)], a_ss.at[s], a_rs.at[s],
            ep_dev((e + 1) % NE),
        )
        done.wait_recv()
        done.wait_send()
        if s == 1:
            done = rcopy(tgo.at[pl.ds(0, n)], tgi.at[pl.ds(0, n)], t_ss, t_rs, ep_dev((e + 1) % NE))
            done.wait_recv()
            done.wait_send()

    def shard(s, shift, core, half):
        col = (((z + shift + 4) % 4) * 2 + core) * COLS
        lo, n = (0, SLOTS) if half is None else (half * HALF, HALF)
        return rows.at[s, pl.ds(lo, n), lanes(col, COLS)]

    GZ = ((1, 0, 0), (1, 0, 1), (-1, 0, 1), (-1, 0, 0), (1, -1, 0), (-1, 1, 1))

    def gz_send(s, k):
        direction, shift, half = GZ[k]
        src = shard(s, shift, c, half)
        return rcopy(src, src, gz_ss.at[s, k], gz_rs.at[s, k], z_dev(direction + 4))

    def gz_wait(s, k):
        direction, shift, half = GZ[k]
        ref = shard(s, shift - direction, c, half)
        rcopy(ref, ref, gz_ss.at[s, k], gz_rs.at[s, k], z_dev(direction + 4)).wait_recv()

    GS = ((0, None), (-1, 0), (1, 1), (-1, 1), (1, 0), (2, 0), (2, 1))

    def gs_send(s, k):
        src = shard(s, GS[k][0], c, GS[k][1])
        return rcopy(src, src, gs_ss.at[s, k], gs_rs.at[s, k], sibling)

    def gs_wait(s, k):
        ref = shard(s, GS[k][0], 1 - c, GS[k][1])
        rcopy(ref, ref, gs_ss.at[s, k], gs_rs.at[s, k], sibling).wait_recv()

    def gather0(s):
        for k in (0, 2, 1, 3):
            gz_send(s, k).start()
        gs_send(s, 0).start()

    def gather1(s):
        gz_wait(s, 0)
        gz_send(s, 4).start()
        gs_send(s, 1).start()
        gz_wait(s, 2)
        gz_send(s, 5).start()
        gs_send(s, 2).start()

    def gather2(s):
        gz_wait(s, 1)
        gs_send(s, 3).start()
        gz_wait(s, 3)
        gs_send(s, 4).start()

    def gather3(s):
        gz_wait(s, 4)
        gs_send(s, 5).start()
        gz_wait(s, 5)
        gs_send(s, 6).start()

    def gather4(s):
        for k in range(7):
            gs_wait(s, k)

    def gather_drain(s):
        for k in range(6):
            gz_send(s, k).wait_send()
        for k in range(7):
            gs_send(s, k).wait_send()

    def silu_mul():
        g = acc[0]
        return g / (1.0 + jnp.exp(-g)) * acc[1]

    def hidden_home(s):
        acc[...] = jnp.zeros_like(acc)

        def body(k, carry):
            x = rows[s, :, lanes(k * 1024, 1024)]
            acc[0] += jnp.dot(x, hw[pl.ds(k * 8, 8)].reshape(1024, 256), preferred_element_type=F32)
            acc[1] += jnp.dot(x, hw[pl.ds(56 + k * 8, 8)].reshape(1024, 256), preferred_element_type=F32)
            return carry

        lax.fori_loop(0, 7, body, 0)
        h = silu_mul()
        if s == 1:
            tag = tgi[...].astype(F32)
            h = h * (1.0 - jnp.concatenate([tag, tag], axis=1))
        hid[s] = h.astype(BF)

    def hidden_copy():
        acc[...] = jnp.zeros_like(acc)
        for dest, first, last in ((0, 0, 21), (0, 21, 28), (1, 28, 42), (1, 42, 56)):
            tree = first // 21

            def body(b, carry, dest=dest, tree=tree):
                x = rows[1, :, lanes((b - 28 * dest) * 256, 256)]
                block = rb[tab[2 * tree], pl.ds(2 * (b - 21 * tree) + tab[2 * tree + 1], 2)]
                acc[dest] += jnp.dot(x, block.reshape(256, 256), preferred_element_type=F32)
                return carry

            lax.fori_loop(first, last, body, 0)
        tag = tgi[...].astype(F32)
        hid[2] = (silu_mul() * jnp.concatenate([tag, tag], axis=1)).astype(BF)

    def block_cols(s, zi, core):
        return lanes((((z + zi) % 4) * 2 + core) * COLS, COLS)

    def sib_copy(s, zi):
        return rcopy(part.at[s, :, block_cols(s, zi, 1 - c)], sibr.at[s, zi], s_ss.at[s, zi], s_rs.at[s, zi], sibling)

    def partials(s):
        for zi in (2, 1, 3, 0):
            zz = (z + zi) % 4

            def body(jj, carry, zz=zz):
                j = zz * 7 + jj
                v = jnp.dot(hid[s], hw[pl.ds(112 + 2 * j, 2)].reshape(256, 256), preferred_element_type=F32)
                if s == 1:
                    first = zz == 0
                    link = jnp.where(first, tab[4], tab[6])
                    t = jnp.where(first, 28 + tab[5], (zz - 1) * 14 + tab[7]) + 2 * jj
                    block = rb[link, pl.ds(t, 2)]
                    v += jnp.dot(hid[2], block.reshape(256, 256), preferred_element_type=F32)
                part[s, :, lanes(j * 256, 256)] = v.astype(BF)
                return carry

            lax.fori_loop(0, 7, body, 0)
            sib_copy(s, zi).start()

    def pair_sum(s, zi):
        return part[s, :, block_cols(s, zi, c)].astype(F32) + sibr[s, zi].astype(F32)

    lo_half, hi_half = pl.ds(0, HALF), pl.ds(HALF, HALF)

    def z_copy(s, k):
        src, dst, direction = (
            (zs.at[s, 0, lo_half], za.at[s], 1),
            (zs.at[s, 0, hi_half], zb.at[s], -1),
            (zs.at[s, 1, hi_half], rp.at[s, hi_half], 1),
            (zs.at[s, 1, lo_half], rp.at[s, lo_half], 1),
            (zs.at[s, 2, lo_half], rm.at[s, lo_half], -1),
            (zs.at[s, 2, hi_half], rm.at[s, hi_half], -1),
        )[k]
        return rcopy(src, dst, z_ss.at[s, k], z_rs.at[s, k], z_dev(direction + 4))

    def reduce1(s):
        sib_copy(s, 2).wait_recv()
        zs[s, 0] = pair_sum(s, 2).astype(BF)
        z_copy(s, 0).start()
        z_copy(s, 1).start()
        sib_copy(s, 1).wait_recv()
        zs[s, 1] = pair_sum(s, 1).astype(BF)
        z_copy(s, 2).start()
        sib_copy(s, 3).wait_recv()
        zs[s, 2] = pair_sum(s, 3).astype(BF)
        z_copy(s, 4).start()

    def reduce2(s):
        z_copy(s, 0).wait_recv()
        zs[s, 1, lo_half] = (zs[s, 1, lo_half].astype(F32) + za[s].astype(F32)).astype(BF)
        z_copy(s, 3).start()
        z_copy(s, 1).wait_recv()
        zs[s, 2, hi_half] = (zs[s, 2, hi_half].astype(F32) + zb[s].astype(F32)).astype(BF)
        z_copy(s, 5).start()

    def reduce3(s):
        sib_copy(s, 0).wait_recv()
        for k in (2, 4, 3, 5):
            z_copy(s, k).wait_recv()
        eo[s] = (pair_sum(s, 0) + rp[s].astype(F32) + rm[s].astype(F32)).astype(BF)

    def reduce_drain(s):
        for zi in range(4):
            sib_copy(s, zi).wait_send()
        for k in range(6):
            z_copy(s, k).wait_send()

    def back_start(s):
        def send(j, carry):
            peer = (e + j) % NE
            rcopy(
                eo.at[s, rows16(peer * CAP, CAP)], ret.at[rows16(s * SLOTS + e * CAP, CAP)],
                r_ss.at[s], r_rs.at[s], ep_dev(peer),
            ).start()
            return carry

        lax.fori_loop(1, NE, send, 0)
        ret[rows16(s * SLOTS + e * CAP, CAP), :] = eo[s, rows16(e * CAP, CAP), :]

    def back_wait(s):
        n = (NE - 1) * CAP
        done = rcopy(
            eo.at[s, pl.ds(0, n)], ret.at[pl.ds(s * SLOTS, n)], r_ss.at[s], r_rs.at[s], ep_dev((e + 1) % NE)
        )
        done.wait_recv()
        done.wait_send()

    def final(j):
        peer = (w + j) % NW
        frm = (w + NW - j) % NW
        return (
            rcopy(outb.at[rows16(peer * 16, 16)], fin.at[w], f_ss.at[j - 1], f_rs.at[j - 1], wide_dev(peer)),
            rcopy(outb.at[rows16(peer * 16, 16)], fin.at[frm], f_ss.at[j - 1], f_rs.at[j - 1], wide_dev(peer)),
        )

    run_slots(2)
    for j in range(1, NW):
        copies = exchange(j)
        copies[2].wait_recv()
        copies[3].wait_recv()
    make_plan()
    a2a_start(0)
    a2a_start(1)
    run_slots(4)
    a2a_wait(0)
    gather0(0)
    run_slots(4)
    gather1(0)
    a2a_wait(1)
    run_slots(3)
    gather2(0)
    gather0(1)
    run_slots(3)
    gather3(0)
    run_slots(1)
    gather4(0)
    hidden_home(0)
    run_slots(2)
    gather1(1)
    partials(0)
    run_slots(2)
    gather2(1)
    reduce1(0)
    run_slots(2)
    gather3(1)
    run_slots(2)
    reduce2(0)
    gather4(1)
    run_slots(2)
    hidden_home(1)
    run_slots(4)
    reduce3(0)
    back_start(0)
    finish_slots()
    hidden_copy()
    partials(1)
    reduce1(1)
    back_wait(0)
    reduce2(1)
    reduce3(1)
    back_start(1)
    back_wait(1)
    outb[...] = jnp.dot(wc[...], ret[...], preferred_element_type=F32).astype(BF)
    for j in range(1, NW):
        final(j)[0].start()
    fin[w] = outb[rows16(w * 16, 16), :]
    for j in range(1, NW):
        copies = exchange(j)
        copies[0].wait_send()
        copies[1].wait_send()
    for s in range(STEPS):
        gather_drain(s)
        reduce_drain(s)
    for j in range(1, NW):
        final(j)[1].wait_recv()
    for k in range(NW):
        out[:, k * COLS : (k + 1) * COLS] = fin[k]
    for j in range(1, NW):
        final(j)[0].wait_send()


def shards(
    requests, routes, gates, replica, placement, copy_plan, capacity, gate_proj, up_proj, down_proj
):
    e = lax.axis_index("ep")
    own = requests.shape[1]
    req = requests.reshape(STEPS * own, D)
    slots = jnp.arange(NE, dtype=jnp.int32)
    home = jnp.sum(jnp.where(slots == copy_plan[0], placement, 0), dtype=jnp.int32)
    cand = (home + jnp.concatenate([jnp.zeros((1,), jnp.int32), copy_plan[1:]])) % NE
    picks = jnp.concatenate(
        [
            routes.astype(F32),
            jnp.broadcast_to(replica.astype(F32)[None], routes.shape),
            gates.astype(F32),
        ],
        axis=2,
    ).reshape(STEPS * own, 6)
    meta = jnp.pad(picks, ((0, 0), (0, 122)))
    par = jnp.concatenate(
        [
            jnp.pad(placement[None].astype(F32), ((0, 0), (0, 112))),
            jnp.pad(cand[None].astype(F32), ((0, 0), (0, 124))),
            jnp.pad(capacity.astype(F32), ((0, 0), (0, 112))),
            jnp.broadcast_to(copy_plan[:1].astype(F32)[None], (1, 128)),
            jnp.zeros((3, 128), F32),
        ],
        axis=0,
    )
    place = ((e // 4 - home // 4) % 4) * 4 + (e % 4 - home % 4) % 4
    at_place = (slots == place)[:, None]
    flag = jnp.sum(jnp.where(at_place, jnp.asarray(FLAGS), 0.0), axis=0)
    tab = jnp.sum(jnp.where(at_place, jnp.asarray(ARRIVE), 0), axis=0, dtype=jnp.int32)

    vmem = pl.BlockSpec(memory_space=pltpu.VMEM)
    smem = pl.BlockSpec(memory_space=pltpu.SMEM)
    hbm = pl.BlockSpec(memory_space=pl.ANY)
    dma = pltpu.SemaphoreType.DMA
    result = pl.pallas_call(
        layer_kernel,
        out_shape=jax.ShapeDtypeStruct((STEPS * own, D), BF),
        in_specs=[vmem, vmem, vmem, smem, smem, hbm, hbm, hbm],
        out_specs=vmem,
        scratch_shapes=[
            pltpu.VMEM((NW, 16, COLS), BF),
            pltpu.VMEM((NW, 16, 128), F32),
            pltpu.VMEM((STEPS, SLOTS, COLS), BF),
            pltpu.VMEM((SLOTS, 128), BF),
            pltpu.VMEM((SLOTS, 128), BF),
            pltpu.VMEM((STEPS, SLOTS, D), BF),
            pltpu.VMEM((168, 128, 256), BF),
            pltpu.VMEM((4, T_SLOTS, 128, 256), BF),
            pltpu.VMEM((4, STAGE, 128, 256), BF),
            pltpu.VMEM((16, 16, 256), BF),
            pltpu.VMEM((2, SLOTS, HID), F32),
            pltpu.VMEM((3, SLOTS, HID), BF),
            pltpu.VMEM((STEPS, SLOTS, D), BF),
            pltpu.VMEM((STEPS, 4, SLOTS, COLS), BF),
            pltpu.VMEM((STEPS, 3, SLOTS, COLS), BF),
            pltpu.VMEM((STEPS, HALF, COLS), BF),
            pltpu.VMEM((STEPS, HALF, COLS), BF),
            pltpu.VMEM((STEPS, SLOTS, COLS), BF),
            pltpu.VMEM((STEPS, SLOTS, COLS), BF),
            pltpu.VMEM((STEPS, SLOTS, COLS), BF),
            pltpu.VMEM((STEPS * SLOTS, COLS), BF),
            pltpu.VMEM((128, STEPS * SLOTS), BF),
            pltpu.VMEM((128, COLS), BF),
            pltpu.VMEM((NW, 16, COLS), BF),
            dma((3,)),
            dma((7,)), dma((7,)), dma((7,)), dma((7,)),
            dma((2,)), dma((2,)), dma, dma, dma,
            dma((4, STAGE)), dma((4, T_SLOTS)),
            dma((2, 6)), dma((2, 6)), dma((2, 7)), dma((2, 7)),
            dma((2, 4)), dma((2, 4)), dma((2, 6)), dma((2, 6)),
            dma((2,)), dma((2,)), dma((7,)), dma((7,)),
        ],
        compiler_params=pltpu.CompilerParams(
            collective_id=0, has_side_effects=True, vmem_limit_bytes=62 * 1024 * 1024
        ),
        name="expert_layer",
    )(
        req, meta, par, flag, tab,
        gate_proj.reshape(56, 128, HID), up_proj.reshape(56, 128, HID), down_proj.reshape(HID, D),
    )
    return result.reshape(STEPS, own, D)


def solution(mesh):
    rows = P(None, ("ep", "wide"), None)
    placed = (
        rows, rows, rows, P(("ep", "wide"), None), P(), P(), P(),
        P("ep", None, "wide"), P("ep", None, "wide"), P("ep", "wide", None),
    )
    return jax.shard_map(shards, mesh=mesh, in_specs=placed, out_specs=rows, check_vma=False)
```

```python
import jax
import jax.numpy as jnp
from jax import lax
from jax.experimental import pallas as pl
from jax.experimental.pallas import tpu as pltpu
from jax.sharding import PartitionSpec as P

BF = jnp.bfloat16
F32 = jnp.float32
STEPS = 2
CAP = 16
NE = 16
NW = 8
GROUP = 64
D = 7168
COLS = D // NW
SLOTS = NE * CAP
HALF = SLOTS // 2
HID = 256

TILES = COLS // 128

STEP_XY = ((1, 0), (-1, 0), (0, 1), (0, -1))
TREES = (
    ((0, 0, 0), (1, 0, 2), (1, 0, 0), (1, 1, 2), (2, 0, 0), (2, 0, 3), (1, 2, 1), (2, 3, 0)),
    ((0, 0, 1), (3, 0, 1), (3, 0, 3), (2, 0, 2), (2, 0, 1), (3, 3, 3), (2, 1, 1), (3, 2, 0)),
    ((0, 0, 2), (0, 1, 1), (0, 1, 0), (0, 1, 2), (3, 1, 3), (1, 1, 3), (3, 1, 2), (3, 2, 2)),
    ((0, 0, 3), (0, 3, 3), (0, 3, 1), (0, 3, 0), (0, 2, 0), (3, 3, 2), (1, 3, 2), (1, 2, 3)),
)
LAG = 3
CHUNKS = 42
FIRST = 28
T_SLOTS = CHUNKS + 3 * LAG
T_STEPS = CHUNKS + 4 * LAG
STAGE = 4
RING = 16


def relay_tables():
    relay, arrive = {}, [{} for _ in TREES]
    for tree, edges in enumerate(TREES):
        came = {(0, 0): (None, 0)}
        for x, y, link in edges:
            via, depth = came[(x, y)]
            to = ((x + STEP_XY[link][0]) % 4, (y + STEP_XY[link][1]) % 4)
            came[to] = (link, depth + 1)
            relay.setdefault((link, link ^ 1 if via is None else via), []).append(y * 4 + x)
            if to in OWNERS:
                arrive[tree].setdefault((link, LAG * depth), []).append(to[1] * 4 + to[0])
    return relay, arrive


OWNERS = ((1, 0), (1, 1), (3, 0), (3, 3), (0, 2))
RELAY, ARRIVE = relay_tables()
MASKS = [("relay", key) for key in sorted(RELAY)] + [
    ("arrive", tree, key) for tree in range(4) for key in sorted(ARRIVE[tree])
]
MASK_AT = {name: i for i, name in enumerate(MASKS)}


def rcopy(src, dst, ssem, rsem, dev):
    return pltpu.make_async_remote_copy(
        src_ref=src,
        dst_ref=dst,
        send_sem=ssem,
        recv_sem=rsem,
        device_id=dev,
        device_id_type=pl.DeviceIdType.MESH,
    )


def lanes(start, size):
    return pl.ds(pl.multiple_of(start, 128), size)


def rows16(start, size):
    return pl.ds(pl.multiple_of(start, 16), size)


def layer_kernel(
    req, routes, gates, replica, placement, copy_plan, capacity, gate, up, down, out,
    xs, meta, xin, xmeta, outg, tgo, tgi, rows, hw, hot, rb, sb, mk, acc, hid, part, sibr, zs, za, zb, rp, rm,
    eo, ret, wc, outb, fin,
    load_sem, x_ss, x_rs, m_ss, m_rs, a_ss, a_rs, t_ss, t_rs,
    b_ss, b_rs, gz_ss, gz_rs, gs_ss, gs_rs, s_ss, s_rs, z_ss, z_rs, r_ss, r_rs, f_ss, f_rs,
):
    e = lax.axis_index("ep")
    w = lax.axis_index("wide")
    ex, ey = e % 4, e // 4
    z, c = w // 2, w % 2

    def wide_dev(other):
        return {"ep": e, "wide": other}

    def ep_dev(other):
        return {"ep": other, "wide": w}

    def z_dev(shift):
        return wide_dev(((z + shift) % 4) * 2 + c)

    sibling = wide_dev(z * 2 + 1 - c)
    link_dev = [
        ep_dev(((ey + dy + 4) % 4) * 4 + (ex + dx + 4) % 4) for dx, dy in STEP_XY
    ]

    def load_weights(j, carry):
        for i, ref in enumerate((gate, up)):
            pltpu.make_async_copy(ref.at[:, j], hw.at[pl.ds(56 * i + TILES * j, TILES)], load_sem).start()
        return carry

    lax.fori_loop(0, NW, load_weights, 0)

    def load_down(j, carry):
        for half in range(2):
            pltpu.make_async_copy(
                down.at[pl.ds(half * 128, 128), lanes(j * 256, 256)], hw.at[112 + 2 * j + half], load_sem
            ).start()
        return carry

    lax.fori_loop(0, 28, load_down, 0)

    barrier = pltpu.get_barrier_semaphore()
    for j in range(1, NW):
        pl.semaphore_signal(barrier, inc=1, device_id=wide_dev((w + j) % NW), device_id_type=pl.DeviceIdType.MESH)
    for j in range(1, NE):
        pl.semaphore_signal(barrier, inc=1, device_id=ep_dev((e + j) % NE), device_id_type=pl.DeviceIdType.MESH)

    both = jnp.concatenate([req[0].astype(F32), req[1].astype(F32)], axis=0).astype(BF)
    for k in range(NW):
        for q in range(TILES):
            xs[k, :, q * 128 : (q + 1) * 128] = both[:, q * 1024 + k * 128 : q * 1024 + (k + 1) * 128]
    lane8 = lax.broadcasted_iota(jnp.int32, (8, 128), 1)
    for s in range(STEPS):
        line = jnp.zeros((8, 128), F32)
        for i, ref in enumerate((routes[s], replica[...], gates[s])):
            values = ref.astype(F32)
            for k in range(2):
                line = jnp.where(lane8 == 2 * i + k, jnp.broadcast_to(values[:, k : k + 1], (8, 128)), line)
        meta[s * 8 : (s + 1) * 8, :] = line

    def spread_row(values):
        line = jnp.zeros((8, 128), jnp.int32)
        for i, value in enumerate(values):
            line = jnp.where(lane8 == i, value, line)
        return jnp.broadcast_to(line[0:1, :].astype(F32), (128, 128))

    home = placement[copy_plan[0]]
    place = ((ey - home // 4 + 4) % 4) * 4 + (ex - home % 4 + 4) % 4
    places = jnp.full((16, 256), place, jnp.int32)
    for i, name in enumerate(MASKS):
        mask = jnp.zeros((16, 256), F32)
        for at in RELAY[name[1]] if name[0] == "relay" else ARRIVE[name[1]][name[2]]:
            mask = jnp.where(places == at, 1.0, mask)
        mk[i] = mask.astype(BF)

    pl.semaphore_wait(barrier, NW - 1 + NE - 1)

    def exchange(j, peer, at):
        return (
            rcopy(xs.at[(w + j) % NW], xin.at[at], x_ss.at[j - 1], x_rs.at[j - 1], wide_dev(peer)),
            rcopy(meta, xmeta.at[at], m_ss.at[j - 1], m_rs.at[j - 1], wide_dev(peer)),
        )

    for j in range(1, NW):
        for copy in reversed(exchange(j, (w + j) % NW, w)):
            copy.start()
    xin[w] = xs[w]
    xmeta[w] = meta[...]
    pltpu.make_async_copy(hw, hw, load_sem).wait()

    def slot_copy(link, t):
        return rcopy(
            sb.at[link, t % STAGE], rb.at[link, t % RING], b_ss.at[link, t % STAGE], b_rs.at[link, t % RING],
            link_dev[link],
        )

    def chunk_at(tree, n, later):
        return 112 + ((n - FIRST) // 2 * 4 + tree) * 2 + n % 2 if later else tree * FIRST + n

    def masked(block, mask):
        return block.reshape(8, 16, 256) * mk[MASK_AT[mask]][None]

    def add(total, term):
        return term if total is None else total + term

    def step(t, own, own_later, recv, wait, send, deliver, deliver_later):
        if recv:
            for link in range(4):
                slot_copy(link, t - LAG).wait_recv()
        if send:
            for link in range(4):
                if wait:
                    slot_copy(link, t - STAGE).wait_send()
                total = None
                for k in range(4):
                    if (link, k) not in RELAY:
                        continue
                    if k == link ^ 1:
                        if own:
                            total = add(total, masked(hw[chunk_at(link, t, own_later)], ("relay", (link, k))))
                    elif recv:
                        total = add(total, masked(rb[k, (t - LAG) % RING], ("relay", (link, k))))
                sb[link, t % STAGE] = total.reshape(128, 256)
                slot_copy(link, t).start()
        if deliver:
            n = t - 4 * LAG
            for tree in range(4):
                total = None
                for link, behind in sorted(ARRIVE[tree]):
                    block = rb[link, (n + behind) % RING]
                    total = add(total, masked(block, ("arrive", tree, (link, behind))))
                hot[chunk_at(tree, n, deliver_later)] = total.reshape(128, 256)

    cursor = [0]

    def run_to(t1):
        t0 = cursor[0]
        t1 = max(t0, min(T_STEPS, t1))
        cursor[0] = t1
        marks = (LAG, STAGE, FIRST, CHUNKS, T_SLOTS, 4 * LAG, 4 * LAG + FIRST)
        cuts = sorted({t0, t1, *[x for x in marks if t0 < x < t1]})
        for lo, hi in zip(cuts[:-1], cuts[1:]):
            kind = (
                lo < CHUNKS, lo >= FIRST, lo >= LAG, lo >= STAGE, lo < T_SLOTS, lo >= 4 * LAG, lo >= 4 * LAG + FIRST
            )
            if hi - lo == 1:
                step(lo, *kind)
            else:
                def body(t, carry, kind=kind):
                    step(t, *kind)
                    return carry

                lax.fori_loop(lo, hi, body, 0)

    def run(count):
        run_to(cursor[0] + count)

    def drain_slots():
        def drain_send(t, carry):
            for link in range(4):
                slot_copy(link, t).wait_send()
            return carry

        lax.fori_loop(T_SLOTS - STAGE, T_SLOTS, drain_send, 0)

    def make_plan():
        picks = xmeta[...].reshape(128, 128)
        lane = lax.broadcasted_iota(jnp.int32, (128, 128), 1)
        line = lax.broadcasted_iota(jnp.int32, (128, 128), 0)
        lane_f = lane.astype(F32)
        second = (line // 8) % 2 == 1
        limits = jnp.where(
            second,
            spread_row([capacity[1, i] for i in range(NE)]),
            spread_row([capacity[0, i] for i in range(NE)]),
        )
        slot_of = spread_row([placement[i] for i in range(NE)])
        cand = spread_row([home] + [(home + copy_plan[i]) % NE for i in range(1, 4)])
        hot_id = jnp.full((128, 128), copy_plan[0], jnp.int32).astype(F32)
        zero = jnp.zeros((128, 128), F32)

        def spread(column):
            return jnp.broadcast_to(picks[:, column : column + 1], (128, 128))

        def total(v):
            return jnp.broadcast_to(jnp.sum(v, axis=1, keepdims=True), (128, 128))

        onehots, servers, copied = [], [], []
        for k in range(2):
            route, pick = spread(k), spread(2 + k)
            server = total(jnp.where(lane_f == route, slot_of, zero))
            chosen = total(jnp.where(lane_f == pick, cand, zero))
            is_hot = jnp.where(second, jnp.where(route == hot_id, 1.0, 0.0), 0.0)
            server = jnp.where(is_hot > 0.5, chosen, server)
            copied.append(jnp.where(pick > 0.5, is_hot, 0.0))
            servers.append(server)
            onehots.append(jnp.where(lane_f == server, 1.0, 0.0))
        earlier = jnp.where(lane < line, 1.0, 0.0) * jnp.where((line // 8) % 2 == (lane // 8) % 2, 1.0, 0.0)
        before = jnp.dot(earlier.astype(BF), (onehots[0] + onehots[1]).astype(BF), preferred_element_type=F32)
        lane_w = lax.broadcasted_iota(jnp.int32, (128, 512), 1).astype(F32)
        base = jnp.where(second, float(SLOTS), 0.0)
        matches = []
        for k in range(2):
            count = before if k == 0 else before + onehots[0]
            position = total(count * onehots[k])
            limit = total(limits * onehots[k])
            column = jnp.where(position < limit, base + servers[k] * CAP + position, -1.0)
            matches.append(jnp.where(lane_w == jnp.broadcast_to(column[:, :1], (128, 512)), 1.0, 0.0))

        def wide512(v):
            return jnp.broadcast_to(v[:, :1], (128, 512))

        wc[...] = (matches[0] * wide512(spread(4)) + matches[1] * wide512(spread(5))).astype(BF)
        dispatch = (matches[0] + matches[1]).astype(BF)
        tags = (matches[0] * wide512(copied[0]) + matches[1] * wide512(copied[1])).astype(BF)
        flat = xin[...].reshape(128, COLS)
        contract = (((0,), (0,)), ((), ()))
        for s in range(STEPS):
            outg[s] = lax.dot_general(
                dispatch[:, s * SLOTS : (s + 1) * SLOTS], flat, contract, preferred_element_type=F32
            ).astype(BF)
        tgo[...] = lax.dot_general(
            tags[:, SLOTS:], jnp.ones((128, 128), BF), contract, preferred_element_type=F32
        ).astype(BF)

    def a2a_start(s):
        def send(j, carry):
            peer = (e + j) % NE
            rcopy(
                outg.at[s, rows16(peer * CAP, CAP)], rows.at[s, rows16(e * CAP, CAP), lanes(w * COLS, COLS)],
                a_ss.at[s], a_rs.at[s], ep_dev(peer),
            ).start()
            if s == 1:
                rcopy(
                    tgo.at[rows16(peer * CAP, CAP)], tgi.at[rows16(e * CAP, CAP)], t_ss, t_rs, ep_dev(peer)
                ).start()
            return carry

        lax.fori_loop(1, NE, send, 0)
        rows[s, rows16(e * CAP, CAP), lanes(w * COLS, COLS)] = outg[s, rows16(e * CAP, CAP), :]
        if s == 1:
            tgi[rows16(e * CAP, CAP), :] = tgo[rows16(e * CAP, CAP), :]

    def a2a_wait(s):
        n = (NE - 1) * CAP
        done = rcopy(
            outg.at[s, pl.ds(0, n)], rows.at[s, pl.ds(0, n), lanes(w * COLS, COLS)], a_ss.at[s], a_rs.at[s],
            ep_dev((e + 1) % NE),
        )
        done.wait_recv()
        done.wait_send()
        if s == 1:
            done = rcopy(tgo.at[pl.ds(0, n)], tgi.at[pl.ds(0, n)], t_ss, t_rs, ep_dev((e + 1) % NE))
            done.wait_recv()
            done.wait_send()

    def shard(s, shift, core, half):
        col = (((z + shift + 4) % 4) * 2 + core) * COLS
        lo, n = (0, SLOTS) if half is None else (half * HALF, HALF)
        return rows.at[s, pl.ds(lo, n), lanes(col, COLS)]

    GZ = ((1, 0, 0), (1, 0, 1), (-1, 0, 1), (-1, 0, 0), (1, -1, 0), (-1, 1, 1))

    def gz_send(s, k):
        direction, shift, half = GZ[k]
        src = shard(s, shift, c, half)
        return rcopy(src, src, gz_ss.at[s, k], gz_rs.at[s, k], z_dev(direction + 4))

    def gz_wait(s, k):
        direction, shift, half = GZ[k]
        ref = shard(s, shift - direction, c, half)
        rcopy(ref, ref, gz_ss.at[s, k], gz_rs.at[s, k], z_dev(direction + 4)).wait_recv()

    GS = ((0, None), (-1, 0), (1, 1), (-1, 1), (1, 0), (2, 0), (2, 1))

    def gs_send(s, k):
        src = shard(s, GS[k][0], c, GS[k][1])
        return rcopy(src, src, gs_ss.at[s, k], gs_rs.at[s, k], sibling)

    def gs_wait(s, k):
        ref = shard(s, GS[k][0], 1 - c, GS[k][1])
        rcopy(ref, ref, gs_ss.at[s, k], gs_rs.at[s, k], sibling).wait_recv()

    def gather0(s):
        for k in (0, 2, 1, 3):
            gz_send(s, k).start()
        gs_send(s, 0).start()

    def gather1(s):
        gz_wait(s, 0)
        gz_send(s, 4).start()
        gs_send(s, 1).start()
        gz_wait(s, 2)
        gz_send(s, 5).start()
        gs_send(s, 2).start()

    def gather2(s):
        gz_wait(s, 1)
        gs_send(s, 3).start()
        gz_wait(s, 3)
        gs_send(s, 4).start()

    def gather3(s):
        gz_wait(s, 4)
        gs_send(s, 5).start()
        gz_wait(s, 5)
        gs_send(s, 6).start()

    def gather4(s):
        for k in range(7):
            gs_wait(s, k)

    def gather_drain(s):
        for k in range(6):
            gz_send(s, k).wait_send()
        for k in range(7):
            gs_send(s, k).wait_send()

    def hidden(s, weights):
        acc[...] = jnp.zeros_like(acc)

        def body(k, carry):
            x = rows[s, :, lanes(k * 1024, 1024)]
            acc[0] += jnp.dot(x, weights[pl.ds(k * 8, 8)].reshape(1024, 256), preferred_element_type=F32)
            acc[1] += jnp.dot(x, weights[pl.ds(56 + k * 8, 8)].reshape(1024, 256), preferred_element_type=F32)
            return carry

        lax.fori_loop(0, 7, body, 0)
        g = acc[0]
        return g / (1.0 + jnp.exp(-g)) * acc[1]

    def copy_tag():
        tag = tgi[...].astype(F32)
        return jnp.concatenate([tag, tag], axis=1)

    PARTS = ((0, 0, TILES), (1, 0, 4), (1, 4, 3))

    def own_cols(p):
        return pl.ds(PARTS[p][1] * 128, PARTS[p][2] * 128)

    def block_cols(p, zi, core):
        return lanes((((z + zi) % 4) * 2 + core) * COLS + PARTS[p][1] * 128, PARTS[p][2] * 128)

    def sib_copy(p, zi):
        s = PARTS[p][0]
        return rcopy(
            part.at[s, :, block_cols(p, zi, 1 - c)], sibr.at[s, zi, :, own_cols(p)],
            s_ss.at[p, zi], s_rs.at[p, zi], sibling,
        )

    def partials(p):
        s, first, count = PARTS[p]
        for zi in (2, 1, 3, 0):
            zz = (z + zi) % 4

            def body(q, carry, zz=zz):
                at = pl.ds(112 + 2 * (q * 4 + zz), 2)
                v = jnp.dot(hid[s], hw[at].reshape(256, 256), preferred_element_type=F32)
                if s == 1:
                    v += jnp.dot(hid[2], hot[at].reshape(256, 256), preferred_element_type=F32)
                v = v.astype(BF)
                for core in range(2):
                    part[s, :, lanes((zz * 2 + core) * COLS + q * 128, 128)] = v[:, core * 128 : (core + 1) * 128]
                return carry

            lax.fori_loop(first, first + count, body, 0)
            sib_copy(p, zi).start()

    def pair_sum(p, zi):
        s = PARTS[p][0]
        return part[s, :, block_cols(p, zi, c)].astype(F32) + sibr[s, zi, :, own_cols(p)].astype(F32)

    lo_half, hi_half = pl.ds(0, HALF), pl.ds(HALF, HALF)

    def z_copy(p, k):
        s, cols = PARTS[p][0], own_cols(p)
        src, dst, direction = (
            (zs.at[s, 0, lo_half, cols], za.at[s, :, cols], 1),
            (zs.at[s, 0, hi_half, cols], zb.at[s, :, cols], -1),
            (zs.at[s, 1, hi_half, cols], rp.at[s, hi_half, cols], 1),
            (zs.at[s, 1, lo_half, cols], rp.at[s, lo_half, cols], 1),
            (zs.at[s, 2, lo_half, cols], rm.at[s, lo_half, cols], -1),
            (zs.at[s, 2, hi_half, cols], rm.at[s, hi_half, cols], -1),
        )[k]
        return rcopy(src, dst, z_ss.at[p, k], z_rs.at[p, k], z_dev(direction + 4))

    def reduce1(p):
        s, cols = PARTS[p][0], own_cols(p)
        sib_copy(p, 2).wait_recv()
        zs[s, 0, :, cols] = pair_sum(p, 2).astype(BF)
        z_copy(p, 0).start()
        z_copy(p, 1).start()
        sib_copy(p, 1).wait_recv()
        zs[s, 1, :, cols] = pair_sum(p, 1).astype(BF)
        z_copy(p, 2).start()
        sib_copy(p, 3).wait_recv()
        zs[s, 2, :, cols] = pair_sum(p, 3).astype(BF)
        z_copy(p, 4).start()

    def reduce2(p):
        s, cols = PARTS[p][0], own_cols(p)
        z_copy(p, 0).wait_recv()
        zs[s, 1, lo_half, cols] = (zs[s, 1, lo_half, cols].astype(F32) + za[s, :, cols].astype(F32)).astype(BF)
        z_copy(p, 3).start()
        z_copy(p, 1).wait_recv()
        zs[s, 2, hi_half, cols] = (zs[s, 2, hi_half, cols].astype(F32) + zb[s, :, cols].astype(F32)).astype(BF)
        z_copy(p, 5).start()

    def reduce3(p):
        s, cols = PARTS[p][0], own_cols(p)
        sib_copy(p, 0).wait_recv()
        for k in (2, 4, 3, 5):
            z_copy(p, k).wait_recv()
        eo[s, :, cols] = (pair_sum(p, 0) + rp[s, :, cols].astype(F32) + rm[s, :, cols].astype(F32)).astype(BF)

    def reduce_drain(p):
        for zi in range(4):
            sib_copy(p, zi).wait_send()
        for k in range(6):
            z_copy(p, k).wait_send()

    def back_start(p):
        s, cols = PARTS[p][0], own_cols(p)

        def send(j, carry):
            peer = (e + j) % NE
            rcopy(
                eo.at[s, rows16(peer * CAP, CAP), cols], ret.at[rows16(s * SLOTS + e * CAP, CAP), cols],
                r_ss.at[p], r_rs.at[p], ep_dev(peer),
            ).start()
            return carry

        lax.fori_loop(1, NE, send, 0)
        ret[rows16(s * SLOTS + e * CAP, CAP), cols] = eo[s, rows16(e * CAP, CAP), cols]

    def back_wait(p):
        s, cols = PARTS[p][0], own_cols(p)
        n = (NE - 1) * CAP
        done = rcopy(
            eo.at[s, pl.ds(0, n), cols], ret.at[pl.ds(s * SLOTS, n), cols], r_ss.at[p], r_rs.at[p],
            ep_dev((e + 1) % NE),
        )
        done.wait_recv()
        done.wait_send()

    def final(p, j, at):
        peer = (w + j) % NW
        cols = own_cols(p)
        return rcopy(
            outb.at[rows16(peer * 16, 16), cols], fin.at[at, :, cols], f_ss.at[p - 1, j - 1], f_rs.at[p - 1, j - 1],
            wide_dev(peer),
        )

    def combine(p):
        cols = own_cols(p)
        outb[:, cols] = jnp.dot(wc[...], ret[:, cols], preferred_element_type=F32).astype(BF)
        for j in range(1, NW):
            final(p, j, w).start()
        fin[w, :, cols] = outb[rows16(w * 16, 16), cols]

    run(3)
    for j in range(1, NW):
        for copy in exchange(j, (w + j) % NW, (w + NW - j) % NW):
            copy.wait_recv()
    make_plan()
    a2a_start(0)
    run(1)
    a2a_start(1)
    run(4)
    a2a_wait(0)
    gather0(0)
    run(3)
    gather1(0)
    a2a_wait(1)
    run(3)
    gather2(0)
    gather0(1)
    run(3)
    gather3(0)
    run(1)
    gather4(0)
    hid[0] = hidden(0, hw).astype(BF)
    run(1)
    gather1(1)
    partials(0)
    run(2)
    gather2(1)
    reduce1(0)
    run(3)
    gather3(1)
    run(1)
    gather4(1)
    reduce2(0)
    run(1)
    hid[1] = (hidden(1, hw) * (1.0 - copy_tag())).astype(BF)
    run(3)
    reduce3(0)
    run_to(4 * LAG + FIRST)
    hid[2] = (hidden(1, hot) * copy_tag()).astype(BF)
    run_to(4 * LAG + FIRST + 8)
    partials(1)
    run(1)
    reduce1(1)
    run(2)
    reduce2(1)
    run(T_STEPS)
    partials(2)
    back_start(0)
    reduce1(2)
    reduce3(1)
    back_start(1)
    reduce2(2)
    back_wait(0)
    back_wait(1)
    combine(1)
    reduce3(2)
    back_start(2)
    drain_slots()
    for j in range(1, NW):
        for copy in exchange(j, (w + j) % NW, w):
            copy.wait_send()
    for s in range(STEPS):
        gather_drain(s)
    for p in range(3):
        reduce_drain(p)
    back_wait(2)
    combine(2)
    for p in (1, 2):
        for j in range(1, NW):
            final(p, j, (w + NW - j) % NW).wait_recv()
    blocks = [fin[k].astype(F32) for k in range(NW)]
    for q in range(TILES):
        line = jnp.concatenate([block[:, q * 128 : (q + 1) * 128] for block in blocks], axis=1)
        for s in range(STEPS):
            out[s, :, q * 1024 : (q + 1) * 1024] = line[s * 8 : (s + 1) * 8].astype(BF)
    for p in (1, 2):
        for j in range(1, NW):
            final(p, j, w).wait_send()


def shards(
    requests, routes, gates, replica, placement, copy_plan, capacity, gate_proj, up_proj, down_proj
):
    vmem = pl.BlockSpec(memory_space=pltpu.VMEM)
    smem = pl.BlockSpec(memory_space=pltpu.SMEM)
    hbm = pl.BlockSpec(memory_space=pl.ANY)
    dma = pltpu.SemaphoreType.DMA
    return pl.pallas_call(
        layer_kernel,
        out_shape=jax.ShapeDtypeStruct(requests.shape, BF),
        in_specs=[vmem, vmem, vmem, vmem, smem, smem, smem, hbm, hbm, hbm],
        out_specs=vmem,
        scratch_shapes=[
            pltpu.VMEM((NW, 16, COLS), BF),
            pltpu.VMEM((16, 128), F32),
            pltpu.VMEM((NW, 16, COLS), BF),
            pltpu.VMEM((NW, 16, 128), F32),
            pltpu.VMEM((STEPS, SLOTS, COLS), BF),
            pltpu.VMEM((SLOTS, 128), BF),
            pltpu.VMEM((SLOTS, 128), BF),
            pltpu.VMEM((STEPS, SLOTS, D), BF),
            pltpu.VMEM((168, 128, 256), BF),
            pltpu.VMEM((168, 128, 256), BF),
            pltpu.VMEM((4, RING, 128, 256), BF),
            pltpu.VMEM((4, STAGE, 128, 256), BF),
            pltpu.VMEM((len(MASKS), 16, 256), BF),
            pltpu.VMEM((2, SLOTS, HID), F32),
            pltpu.VMEM((3, SLOTS, HID), BF),
            pltpu.VMEM((STEPS, SLOTS, D), BF),
            pltpu.VMEM((STEPS, 4, SLOTS, COLS), BF),
            pltpu.VMEM((STEPS, 3, SLOTS, COLS), BF),
            pltpu.VMEM((STEPS, HALF, COLS), BF),
            pltpu.VMEM((STEPS, HALF, COLS), BF),
            pltpu.VMEM((STEPS, SLOTS, COLS), BF),
            pltpu.VMEM((STEPS, SLOTS, COLS), BF),
            pltpu.VMEM((STEPS, SLOTS, COLS), BF),
            pltpu.VMEM((STEPS * SLOTS, COLS), BF),
            pltpu.VMEM((128, STEPS * SLOTS), BF),
            pltpu.VMEM((128, COLS), BF),
            pltpu.VMEM((NW, 16, COLS), BF),
            dma,
            dma((7,)), dma((7,)), dma((7,)), dma((7,)),
            dma((2,)), dma((2,)), dma, dma,
            dma((4, STAGE)), dma((4, RING)),
            dma((2, 6)), dma((2, 6)), dma((2, 7)), dma((2, 7)),
            dma((3, 4)), dma((3, 4)), dma((3, 6)), dma((3, 6)),
            dma((3,)), dma((3,)), dma((2, 7)), dma((2, 7)),
        ],
        compiler_params=pltpu.CompilerParams(
            collective_id=0, has_side_effects=True, vmem_limit_bytes=62 * 1024 * 1024
        ),
        name="expert_layer",
    )(
        requests, routes, gates, replica, placement, copy_plan, capacity,
        gate_proj.reshape(TILES, NW, 128, HID), up_proj.reshape(TILES, NW, 128, HID), down_proj.reshape(HID, D),
    )


def solution(mesh):
    rows = P(None, ("ep", "wide"), None)
    placed = (
        rows, rows, rows, P(("ep", "wide"), None), P(), P(), P(),
        P("ep", None, "wide"), P("ep", None, "wide"), P("ep", "wide", None),
    )
    return jax.shard_map(shards, mesh=mesh, in_specs=placed, out_specs=rows, check_vma=False)
```

```python
import jax
import jax.numpy as jnp
from jax import lax
from jax.experimental import pallas as pl
from jax.experimental.pallas import tpu as pltpu
from jax.sharding import PartitionSpec as P

BF = jnp.bfloat16
F32 = jnp.float32
STEPS = 2
CAP = 16
NE = 16
NW = 8
GROUP = 64
D = 7168
COLS = D // NW
SLOTS = NE * CAP
HALF = SLOTS // 2
HID = 256

TILES = COLS // 128

STEP_XY = ((1, 0), (-1, 0), (0, 1), (0, -1))
TREES = (
    ((0, 0, 0), (1, 0, 2), (1, 0, 0), (1, 1, 2), (2, 0, 0), (2, 0, 3), (1, 2, 1), (2, 3, 0)),
    ((0, 0, 1), (3, 0, 1), (3, 0, 3), (2, 0, 2), (2, 0, 1), (3, 3, 3), (2, 1, 1), (3, 2, 0)),
    ((0, 0, 2), (0, 1, 1), (0, 1, 0), (0, 1, 2), (3, 1, 3), (1, 1, 3), (3, 1, 2), (3, 2, 2)),
    ((0, 0, 3), (0, 3, 3), (0, 3, 1), (0, 3, 0), (0, 2, 0), (3, 3, 2), (1, 3, 2), (1, 2, 3)),
)
LAG = 3
CHUNKS = 42
FIRST = 28
T_SLOTS = CHUNKS + 3 * LAG
T_STEPS = CHUNKS + 4 * LAG
STAGE = 4
RING = 16


def relay_tables():
    relay, arrive = {}, [{} for _ in TREES]
    for tree, edges in enumerate(TREES):
        came = {(0, 0): (None, 0)}
        for x, y, link in edges:
            via, depth = came[(x, y)]
            to = ((x + STEP_XY[link][0]) % 4, (y + STEP_XY[link][1]) % 4)
            came[to] = (link, depth + 1)
            relay.setdefault((link, link ^ 1 if via is None else via), []).append(y * 4 + x)
            if to in OWNERS:
                arrive[tree].setdefault((link, LAG * depth), []).append(to[1] * 4 + to[0])
    return relay, arrive


OWNERS = ((1, 0), (1, 1), (3, 0), (3, 3), (0, 2))
RELAY, ARRIVE = relay_tables()
MASKS = [("relay", key) for key in sorted(RELAY)] + [
    ("arrive", tree, key) for tree in range(4) for key in sorted(ARRIVE[tree])
]
MASK_AT = {name: i for i, name in enumerate(MASKS)}


def rcopy(src, dst, ssem, rsem, dev):
    return pltpu.make_async_remote_copy(
        src_ref=src,
        dst_ref=dst,
        send_sem=ssem,
        recv_sem=rsem,
        device_id=dev,
        device_id_type=pl.DeviceIdType.MESH,
    )


def lanes(start, size):
    return pl.ds(pl.multiple_of(start, 128), size)


def rows16(start, size):
    return pl.ds(pl.multiple_of(start, 16), size)


def layer_kernel(
    req, routes, gates, replica, placement, copy_plan, capacity, gate, up, down, out,
    xs, meta, xin, xmeta, outg, tgo, tgi, rows, hw, hot, rb, sb, mk, acc, hid, part, sibr, zs, za, zb, rp, rm,
    eo, ret, wc, outb, fin,
    load_sem, x_ss, x_rs, m_ss, m_rs, a_ss, a_rs, t_ss, t_rs,
    b_ss, b_rs, gz_ss, gz_rs, gs_ss, gs_rs, s_ss, s_rs, z_ss, z_rs, r_ss, r_rs, f_ss, f_rs,
):
    e = lax.axis_index("ep")
    w = lax.axis_index("wide")
    ex, ey = e % 4, e // 4
    z, c = w // 2, w % 2

    def wide_dev(other):
        return {"ep": e, "wide": other}

    def ep_dev(other):
        return {"ep": other, "wide": w}

    def z_dev(shift):
        return wide_dev(((z + shift) % 4) * 2 + c)

    sibling = wide_dev(z * 2 + 1 - c)
    link_dev = [
        ep_dev(((ey + dy + 4) % 4) * 4 + (ex + dx + 4) % 4) for dx, dy in STEP_XY
    ]

    def load_weights(j, carry):
        for i, ref in enumerate((gate, up)):
            pltpu.make_async_copy(ref.at[:, j], hw.at[pl.ds(56 * i + TILES * j, TILES)], load_sem).start()
        return carry

    lax.fori_loop(0, NW, load_weights, 0)

    def load_down(j, carry):
        for half in range(2):
            pltpu.make_async_copy(
                down.at[pl.ds(half * 128, 128), lanes(j * 256, 256)], hw.at[112 + 2 * j + half], load_sem
            ).start()
        return carry

    lax.fori_loop(0, 28, load_down, 0)

    barrier = pltpu.get_barrier_semaphore()
    for j in range(1, NW):
        pl.semaphore_signal(barrier, inc=1, device_id=wide_dev((w + j) % NW), device_id_type=pl.DeviceIdType.MESH)
    for j in range(1, NE):
        pl.semaphore_signal(barrier, inc=1, device_id=ep_dev((e + j) % NE), device_id_type=pl.DeviceIdType.MESH)

    both = jnp.concatenate([req[0].astype(F32), req[1].astype(F32)], axis=0).astype(BF)
    for k in range(NW):
        for q in range(TILES):
            xs[k, :, q * 128 : (q + 1) * 128] = both[:, q * 1024 + k * 128 : q * 1024 + (k + 1) * 128]
    lane8 = lax.broadcasted_iota(jnp.int32, (8, 128), 1)
    for s in range(STEPS):
        line = jnp.zeros((8, 128), F32)
        for i, ref in enumerate((routes[s], replica[...], gates[s])):
            values = ref.astype(F32).T
            for k in range(2):
                line = jnp.where(lane8 == 2 * i + k, jnp.broadcast_to(values[:, k : k + 1], (8, 128)), line)
        meta[s * 8 : (s + 1) * 8, :] = line

    def spread_row(values):
        line = jnp.zeros((8, 128), jnp.int32)
        for i, value in enumerate(values):
            line = jnp.where(lane8 == i, value, line)
        return jnp.broadcast_to(line[0:1, :].astype(F32), (128, 128))

    home = placement[copy_plan[0]]
    place = ((ey - home // 4 + 4) % 4) * 4 + (ex - home % 4 + 4) % 4
    places = jnp.full((16, 256), place, jnp.int32)
    for i, name in enumerate(MASKS):
        mask = jnp.zeros((16, 256), F32)
        for at in RELAY[name[1]] if name[0] == "relay" else ARRIVE[name[1]][name[2]]:
            mask = jnp.where(places == at, 1.0, mask)
        mk[i] = mask.astype(BF)

    pl.semaphore_wait(barrier, NW - 1 + NE - 1)

    def exchange(j, peer, at):
        return (
            rcopy(xs.at[(w + j) % NW], xin.at[at], x_ss.at[j - 1], x_rs.at[j - 1], wide_dev(peer)),
            rcopy(meta, xmeta.at[at], m_ss.at[j - 1], m_rs.at[j - 1], wide_dev(peer)),
        )

    for j in range(1, NW):
        for copy in reversed(exchange(j, (w + j) % NW, w)):
            copy.start()
    xin[w] = xs[w]
    xmeta[w] = meta[...]
    pltpu.make_async_copy(hw, hw, load_sem).wait()

    def slot_copy(link, t):
        return rcopy(
            sb.at[link, t % STAGE], rb.at[link, t % RING], b_ss.at[link, t % STAGE], b_rs.at[link, t % RING],
            link_dev[link],
        )

    def chunk_at(tree, n, later):
        return 112 + ((n - FIRST) // 2 * 4 + tree) * 2 + n % 2 if later else tree * FIRST + n

    def masked(block, mask):
        return block.reshape(8, 16, 256) * mk[MASK_AT[mask]][None]

    def add(total, term):
        return term if total is None else total + term

    def step(t, own, own_later, recv, wait, send, deliver, deliver_later):
        if recv:
            for link in range(4):
                slot_copy(link, t - LAG).wait_recv()
        if send:
            for link in range(4):
                if wait:
                    slot_copy(link, t - STAGE).wait_send()
                total = None
                for k in range(4):
                    if (link, k) not in RELAY:
                        continue
                    if k == link ^ 1:
                        if own:
                            total = add(total, masked(hw[chunk_at(link, t, own_later)], ("relay", (link, k))))
                    elif recv:
                        total = add(total, masked(rb[k, (t - LAG) % RING], ("relay", (link, k))))
                sb[link, t % STAGE] = total.reshape(128, 256)
                slot_copy(link, t).start()
        if deliver:
            n = t - 4 * LAG
            for tree in range(4):
                total = None
                for link, behind in sorted(ARRIVE[tree]):
                    block = rb[link, (n + behind) % RING]
                    total = add(total, masked(block, ("arrive", tree, (link, behind))))
                hot[chunk_at(tree, n, deliver_later)] = total.reshape(128, 256)

    cursor = [0]

    def run_to(t1):
        t0 = cursor[0]
        t1 = max(t0, min(T_STEPS, t1))
        cursor[0] = t1
        marks = (LAG, STAGE, FIRST, CHUNKS, T_SLOTS, 4 * LAG, 4 * LAG + FIRST)
        cuts = sorted({t0, t1, *[x for x in marks if t0 < x < t1]})
        for lo, hi in zip(cuts[:-1], cuts[1:]):
            kind = (
                lo < CHUNKS, lo >= FIRST, lo >= LAG, lo >= STAGE, lo < T_SLOTS, lo >= 4 * LAG, lo >= 4 * LAG + FIRST
            )
            if hi - lo == 1:
                step(lo, *kind)
            else:
                def body(t, carry, kind=kind):
                    step(t, *kind)
                    return carry

                lax.fori_loop(lo, hi, body, 0)

    def run(count):
        run_to(cursor[0] + count)

    def drain_slots():
        def drain_send(t, carry):
            for link in range(4):
                slot_copy(link, t).wait_send()
            return carry

        lax.fori_loop(T_SLOTS - STAGE, T_SLOTS, drain_send, 0)

    def make_plan():
        picks = xmeta[...].reshape(128, 128)
        lane = lax.broadcasted_iota(jnp.int32, (128, 128), 1)
        line = lax.broadcasted_iota(jnp.int32, (128, 128), 0)
        lane_f = lane.astype(F32)
        second = (line // 8) % 2 == 1
        limits = jnp.where(
            second,
            spread_row([capacity[1, i] for i in range(NE)]),
            spread_row([capacity[0, i] for i in range(NE)]),
        )
        slot_of = spread_row([placement[i] for i in range(NE)])
        cand = spread_row([home] + [(home + copy_plan[i]) % NE for i in range(1, 4)])
        hot_id = jnp.full((128, 128), copy_plan[0], jnp.int32).astype(F32)
        zero = jnp.zeros((128, 128), F32)

        def spread(column):
            return jnp.broadcast_to(picks[:, column : column + 1], (128, 128))

        def total(v):
            return jnp.broadcast_to(jnp.sum(v, axis=1, keepdims=True), (128, 128))

        onehots, servers, copied = [], [], []
        for k in range(2):
            route, pick = spread(k), spread(2 + k)
            server = total(jnp.where(lane_f == route, slot_of, zero))
            chosen = total(jnp.where(lane_f == pick, cand, zero))
            is_hot = jnp.where(second, jnp.where(route == hot_id, 1.0, 0.0), 0.0)
            server = jnp.where(is_hot > 0.5, chosen, server)
            copied.append(jnp.where(pick > 0.5, is_hot, 0.0))
            servers.append(server)
            onehots.append(jnp.where(lane_f == server, 1.0, 0.0))
        earlier = jnp.where(lane < line, 1.0, 0.0) * jnp.where((line // 8) % 2 == (lane // 8) % 2, 1.0, 0.0)
        before = jnp.dot(earlier.astype(BF), (onehots[0] + onehots[1]).astype(BF), preferred_element_type=F32)
        lane_w = lax.broadcasted_iota(jnp.int32, (128, 512), 1).astype(F32)
        base = jnp.where(second, float(SLOTS), 0.0)
        matches = []
        for k in range(2):
            count = before if k == 0 else before + onehots[0]
            position = total(count * onehots[k])
            limit = total(limits * onehots[k])
            column = jnp.where(position < limit, base + servers[k] * CAP + position, -1.0)
            matches.append(jnp.where(lane_w == jnp.broadcast_to(column[:, :1], (128, 512)), 1.0, 0.0))

        def wide512(v):
            return jnp.broadcast_to(v[:, :1], (128, 512))

        wc[...] = (matches[0] * wide512(spread(4)) + matches[1] * wide512(spread(5))).astype(BF)
        dispatch = (matches[0] + matches[1]).astype(BF)
        tags = (matches[0] * wide512(copied[0]) + matches[1] * wide512(copied[1])).astype(BF)
        flat = xin[...].reshape(128, COLS)
        contract = (((0,), (0,)), ((), ()))
        for s in range(STEPS):
            outg[s] = lax.dot_general(
                dispatch[:, s * SLOTS : (s + 1) * SLOTS], flat, contract, preferred_element_type=F32
            ).astype(BF)
        tgo[...] = lax.dot_general(
            tags[:, SLOTS:], jnp.ones((128, 128), BF), contract, preferred_element_type=F32
        ).astype(BF)

    def a2a_start(s):
        def send(j, carry):
            peer = (e + j) % NE
            rcopy(
                outg.at[s, rows16(peer * CAP, CAP)], rows.at[s, rows16(e * CAP, CAP), lanes(w * COLS, COLS)],
                a_ss.at[s], a_rs.at[s], ep_dev(peer),
            ).start()
            if s == 1:
                rcopy(
                    tgo.at[rows16(peer * CAP, CAP)], tgi.at[rows16(e * CAP, CAP)], t_ss, t_rs, ep_dev(peer)
                ).start()
            return carry

        lax.fori_loop(1, NE, send, 0)
        rows[s, rows16(e * CAP, CAP), lanes(w * COLS, COLS)] = outg[s, rows16(e * CAP, CAP), :]
        if s == 1:
            tgi[rows16(e * CAP, CAP), :] = tgo[rows16(e * CAP, CAP), :]

    def a2a_wait(s):
        n = (NE - 1) * CAP
        done = rcopy(
            outg.at[s, pl.ds(0, n)], rows.at[s, pl.ds(0, n), lanes(w * COLS, COLS)], a_ss.at[s], a_rs.at[s],
            ep_dev((e + 1) % NE),
        )
        done.wait_recv()
        done.wait_send()
        if s == 1:
            done = rcopy(tgo.at[pl.ds(0, n)], tgi.at[pl.ds(0, n)], t_ss, t_rs, ep_dev((e + 1) % NE))
            done.wait_recv()
            done.wait_send()

    def shard(s, shift, core, half):
        col = (((z + shift + 4) % 4) * 2 + core) * COLS
        lo, n = (0, SLOTS) if half is None else (half * HALF, HALF)
        return rows.at[s, pl.ds(lo, n), lanes(col, COLS)]

    GZ = ((1, 0, 0), (1, 0, 1), (-1, 0, 1), (-1, 0, 0), (1, -1, 0), (-1, 1, 1))

    def gz_send(s, k):
        direction, shift, half = GZ[k]
        src = shard(s, shift, c, half)
        return rcopy(src, src, gz_ss.at[s, k], gz_rs.at[s, k], z_dev(direction + 4))

    def gz_wait(s, k):
        direction, shift, half = GZ[k]
        ref = shard(s, shift - direction, c, half)
        rcopy(ref, ref, gz_ss.at[s, k], gz_rs.at[s, k], z_dev(direction + 4)).wait_recv()

    GS = ((0, None), (-1, 0), (1, 1), (-1, 1), (1, 0), (2, 0), (2, 1))

    def gs_send(s, k):
        src = shard(s, GS[k][0], c, GS[k][1])
        return rcopy(src, src, gs_ss.at[s, k], gs_rs.at[s, k], sibling)

    def gs_wait(s, k):
        ref = shard(s, GS[k][0], 1 - c, GS[k][1])
        rcopy(ref, ref, gs_ss.at[s, k], gs_rs.at[s, k], sibling).wait_recv()

    def gather0(s):
        for k in (0, 2, 1, 3):
            gz_send(s, k).start()
        gs_send(s, 0).start()

    def gather1(s):
        gz_wait(s, 0)
        gz_send(s, 4).start()
        gs_send(s, 1).start()
        gz_wait(s, 2)
        gz_send(s, 5).start()
        gs_send(s, 2).start()

    def gather2(s):
        gz_wait(s, 1)
        gs_send(s, 3).start()
        gz_wait(s, 3)
        gs_send(s, 4).start()

    def gather3(s):
        gz_wait(s, 4)
        gs_send(s, 5).start()
        gz_wait(s, 5)
        gs_send(s, 6).start()

    def gather4(s):
        for k in range(7):
            gs_wait(s, k)

    def gather_drain(s):
        for k in range(6):
            gz_send(s, k).wait_send()
        for k in range(7):
            gs_send(s, k).wait_send()

    def hidden(s, weights, slots):
        acc[...] = jnp.zeros_like(acc)

        def body(k, carry):
            x = rows[s, :, lanes(k * 1024, 1024)]
            acc[0] += jnp.dot(x, weights[pl.ds(k * 8, 8)].reshape(1024, 256), preferred_element_type=F32)
            acc[1] += jnp.dot(x, weights[pl.ds(56 + k * 8, 8)].reshape(1024, 256), preferred_element_type=F32)
            return carry

        for lo, hi in ((0, 2), (2, 4), (4, 6), (6, 7)):
            lax.fori_loop(lo, hi, body, 0)
            run(slots)
        g = acc[0]
        return g / (1.0 + jnp.exp(-g)) * acc[1]

    def copy_tag():
        tag = tgi[...].astype(F32)
        return jnp.concatenate([tag, tag], axis=1)

    PARTS = ((0, 0, TILES), (1, 0, 3), (1, 3, 3), (1, 6, 1))

    def own_cols(p):
        return pl.ds(PARTS[p][1] * 128, PARTS[p][2] * 128)

    def block_cols(p, zi, core):
        return lanes((((z + zi) % 4) * 2 + core) * COLS + PARTS[p][1] * 128, PARTS[p][2] * 128)

    def sib_copy(p, zi):
        s = PARTS[p][0]
        return rcopy(
            part.at[s, :, block_cols(p, zi, 1 - c)], sibr.at[s, zi, :, own_cols(p)],
            s_ss.at[p, zi], s_rs.at[p, zi], sibling,
        )

    def partials(p, slots):
        s, first, count = PARTS[p]
        for zi in (2, 1, 3, 0):
            zz = (z + zi) % 4
            for q in range(first, first + count):
                at = pl.ds(112 + 2 * (q * 4 + zz), 2)
                v = jnp.dot(hid[s], hw[at].reshape(256, 256), preferred_element_type=F32)
                if s == 1:
                    v += jnp.dot(hid[2], hot[at].reshape(256, 256), preferred_element_type=F32)
                v = v.astype(BF)
                for core in range(2):
                    part[s, :, lanes((zz * 2 + core) * COLS + q * 128, 128)] = v[:, core * 128 : (core + 1) * 128]
            sib_copy(p, zi).start()
            run(slots)

    def pair_sum(p, zi):
        s = PARTS[p][0]
        return part[s, :, block_cols(p, zi, c)].astype(F32) + sibr[s, zi, :, own_cols(p)].astype(F32)

    lo_half, hi_half = pl.ds(0, HALF), pl.ds(HALF, HALF)

    def z_copy(p, k):
        s, cols = PARTS[p][0], own_cols(p)
        src, dst, direction = (
            (zs.at[s, 0, lo_half, cols], za.at[s, :, cols], 1),
            (zs.at[s, 0, hi_half, cols], zb.at[s, :, cols], -1),
            (zs.at[s, 1, hi_half, cols], rp.at[s, hi_half, cols], 1),
            (zs.at[s, 1, lo_half, cols], rp.at[s, lo_half, cols], 1),
            (zs.at[s, 2, lo_half, cols], rm.at[s, lo_half, cols], -1),
            (zs.at[s, 2, hi_half, cols], rm.at[s, hi_half, cols], -1),
        )[k]
        return rcopy(src, dst, z_ss.at[p, k], z_rs.at[p, k], z_dev(direction + 4))

    def reduce1(p):
        s, cols = PARTS[p][0], own_cols(p)
        sib_copy(p, 2).wait_recv()
        zs[s, 0, :, cols] = pair_sum(p, 2).astype(BF)
        z_copy(p, 0).start()
        z_copy(p, 1).start()
        sib_copy(p, 1).wait_recv()
        zs[s, 1, :, cols] = pair_sum(p, 1).astype(BF)
        z_copy(p, 2).start()
        sib_copy(p, 3).wait_recv()
        zs[s, 2, :, cols] = pair_sum(p, 3).astype(BF)
        z_copy(p, 4).start()

    def reduce2(p):
        s, cols = PARTS[p][0], own_cols(p)
        z_copy(p, 0).wait_recv()
        zs[s, 1, lo_half, cols] = (zs[s, 1, lo_half, cols].astype(F32) + za[s, :, cols].astype(F32)).astype(BF)
        z_copy(p, 3).start()
        z_copy(p, 1).wait_recv()
        zs[s, 2, hi_half, cols] = (zs[s, 2, hi_half, cols].astype(F32) + zb[s, :, cols].astype(F32)).astype(BF)
        z_copy(p, 5).start()

    def reduce3(p):
        s, cols = PARTS[p][0], own_cols(p)
        sib_copy(p, 0).wait_recv()
        for k in (2, 4, 3, 5):
            z_copy(p, k).wait_recv()
        eo[s, :, cols] = (pair_sum(p, 0) + rp[s, :, cols].astype(F32) + rm[s, :, cols].astype(F32)).astype(BF)

    def reduce_drain(p):
        for zi in range(4):
            sib_copy(p, zi).wait_send()
        for k in range(6):
            z_copy(p, k).wait_send()

    def back_start(p):
        s, cols = PARTS[p][0], own_cols(p)

        def send(j, carry):
            peer = (e + j) % NE
            rcopy(
                eo.at[s, rows16(peer * CAP, CAP), cols], ret.at[rows16(s * SLOTS + e * CAP, CAP), cols],
                r_ss.at[p], r_rs.at[p], ep_dev(peer),
            ).start()
            return carry

        lax.fori_loop(1, NE, send, 0)
        ret[rows16(s * SLOTS + e * CAP, CAP), cols] = eo[s, rows16(e * CAP, CAP), cols]

    def back_wait(p):
        s, cols = PARTS[p][0], own_cols(p)
        n = (NE - 1) * CAP
        done = rcopy(
            eo.at[s, pl.ds(0, n), cols], ret.at[pl.ds(s * SLOTS, n), cols], r_ss.at[p], r_rs.at[p],
            ep_dev((e + 1) % NE),
        )
        done.wait_recv()
        done.wait_send()

    def final(p, j, at):
        peer = (w + j) % NW
        cols = own_cols(p)
        return rcopy(
            outb.at[rows16(peer * 16, 16), cols], fin.at[at, :, cols], f_ss.at[p - 1, j - 1], f_rs.at[p - 1, j - 1],
            wide_dev(peer),
        )

    def combine(p):
        cols = own_cols(p)
        outb[:, cols] = jnp.dot(wc[...], ret[:, cols], preferred_element_type=F32).astype(BF)
        for j in range(1, NW):
            final(p, j, w).start()
        fin[w, :, cols] = outb[rows16(w * 16, 16), cols]

    run(3)
    for j in range(1, NW):
        for copy in exchange(j, (w + j) % NW, (w + NW - j) % NW):
            copy.wait_recv()
    make_plan()
    a2a_start(0)
    run(1)
    a2a_start(1)
    run_to(9)
    a2a_wait(0)
    gather0(0)
    run_to(13)
    gather1(0)
    a2a_wait(1)
    run_to(17)
    gather2(0)
    gather0(1)
    run_to(20)
    gather3(0)
    run_to(21)
    gather4(0)
    hid[0] = hidden(0, hw, 1).astype(BF)
    gather1(1)
    partials(0, 1)
    gather2(1)
    reduce1(0)
    run_to(32)
    gather3(1)
    run_to(33)
    gather4(1)
    hid[1] = (hidden(1, hw, 1) * (1.0 - copy_tag())).astype(BF)
    reduce2(0)
    run_to(4 * LAG + FIRST)
    hid[2] = (hidden(1, hot, 1) * copy_tag()).astype(BF)
    reduce3(0)
    run_to(4 * LAG + FIRST + 6)
    partials(1, 0)
    run(2)
    reduce1(1)
    run(2)
    reduce2(1)
    run_to(4 * LAG + FIRST + 12)
    partials(2, 0)
    run(T_STEPS)
    reduce1(2)
    partials(3, 0)
    reduce3(1)
    back_start(0)
    back_start(1)
    reduce2(2)
    reduce1(3)
    reduce2(3)
    reduce3(2)
    back_start(2)
    back_wait(0)
    back_wait(1)
    combine(1)
    reduce3(3)
    back_start(3)
    back_wait(2)
    combine(2)
    drain_slots()
    for j in range(1, NW):
        for copy in exchange(j, (w + j) % NW, w):
            copy.wait_send()
    for s in range(STEPS):
        gather_drain(s)
    for p in range(4):
        reduce_drain(p)
    back_wait(3)
    combine(3)
    for p in (1, 2, 3):
        for j in range(1, NW):
            final(p, j, (w + NW - j) % NW).wait_recv()
    blocks = [fin[k].astype(F32) for k in range(NW)]
    for q in range(TILES):
        line = jnp.concatenate([block[:, q * 128 : (q + 1) * 128] for block in blocks], axis=1)
        for s in range(STEPS):
            out[s, :, q * 1024 : (q + 1) * 1024] = line[s * 8 : (s + 1) * 8].astype(BF)
    for p in (1, 2, 3):
        for j in range(1, NW):
            final(p, j, w).wait_send()


def shards(
    requests, routes, gates, replica, placement, copy_plan, capacity, gate_proj, up_proj, down_proj
):
    vmem = pl.BlockSpec(memory_space=pltpu.VMEM)
    smem = pl.BlockSpec(memory_space=pltpu.SMEM)
    hbm = pl.BlockSpec(memory_space=pl.ANY)
    dma = pltpu.SemaphoreType.DMA
    return pl.pallas_call(
        layer_kernel,
        out_shape=jax.ShapeDtypeStruct(requests.shape, BF),
        in_specs=[vmem, vmem, vmem, vmem, smem, smem, smem, hbm, hbm, hbm],
        out_specs=vmem,
        scratch_shapes=[
            pltpu.VMEM((NW, 16, COLS), BF),
            pltpu.VMEM((16, 128), F32),
            pltpu.VMEM((NW, 16, COLS), BF),
            pltpu.VMEM((NW, 16, 128), F32),
            pltpu.VMEM((STEPS, SLOTS, COLS), BF),
            pltpu.VMEM((SLOTS, 128), BF),
            pltpu.VMEM((SLOTS, 128), BF),
            pltpu.VMEM((STEPS, SLOTS, D), BF),
            pltpu.VMEM((168, 128, 256), BF),
            pltpu.VMEM((168, 128, 256), BF),
            pltpu.VMEM((4, RING, 128, 256), BF),
            pltpu.VMEM((4, STAGE, 128, 256), BF),
            pltpu.VMEM((len(MASKS), 16, 256), BF),
            pltpu.VMEM((2, SLOTS, HID), F32),
            pltpu.VMEM((3, SLOTS, HID), BF),
            pltpu.VMEM((STEPS, SLOTS, D), BF),
            pltpu.VMEM((STEPS, 4, SLOTS, COLS), BF),
            pltpu.VMEM((STEPS, 3, SLOTS, COLS), BF),
            pltpu.VMEM((STEPS, HALF, COLS), BF),
            pltpu.VMEM((STEPS, HALF, COLS), BF),
            pltpu.VMEM((STEPS, SLOTS, COLS), BF),
            pltpu.VMEM((STEPS, SLOTS, COLS), BF),
            pltpu.VMEM((STEPS, SLOTS, COLS), BF),
            pltpu.VMEM((STEPS * SLOTS, COLS), BF),
            pltpu.VMEM((128, STEPS * SLOTS), BF),
            pltpu.VMEM((128, COLS), BF),
            pltpu.VMEM((NW, 16, COLS), BF),
            dma,
            dma((7,)), dma((7,)), dma((7,)), dma((7,)),
            dma((2,)), dma((2,)), dma, dma,
            dma((4, STAGE)), dma((4, RING)),
            dma((2, 6)), dma((2, 6)), dma((2, 7)), dma((2, 7)),
            dma((4, 4)), dma((4, 4)), dma((4, 6)), dma((4, 6)),
            dma((4,)), dma((4,)), dma((3, 7)), dma((3, 7)),
        ],
        compiler_params=pltpu.CompilerParams(
            collective_id=0, has_side_effects=True, vmem_limit_bytes=62 * 1024 * 1024
        ),
        name="expert_layer",
    )(
        requests, jnp.swapaxes(routes, 1, 2), jnp.swapaxes(gates, 1, 2), replica.T, placement, copy_plan, capacity,
        gate_proj.reshape(TILES, NW, 128, HID), up_proj.reshape(TILES, NW, 128, HID), down_proj.reshape(HID, D),
    )


def solution(mesh):
    rows = P(None, ("ep", "wide"), None)
    placed = (
        rows, rows, rows, P(("ep", "wide"), None), P(), P(), P(),
        P("ep", None, "wide"), P("ep", None, "wide"), P("ep", "wide", None),
    )
    return jax.shard_map(shards, mesh=mesh, in_specs=placed, out_specs=rows, check_vma=False)
```

```python
import jax
import jax.numpy as jnp
from jax import lax
from jax.experimental import pallas as pl
from jax.experimental.pallas import tpu as pltpu
from jax.sharding import PartitionSpec as P

BF = jnp.bfloat16
F32 = jnp.float32
STEPS = 2
CAP = 16
NE = 16
NW = 8
GROUP = 64
D = 7168
COLS = D // NW
SLOTS = NE * CAP
HALF = SLOTS // 2
HID = 256

TILES = COLS // 128

STEP_XY = ((1, 0), (-1, 0), (0, 1), (0, -1))
TREES = (
    ((0, 0, 0), (1, 0, 2), (1, 0, 0), (1, 1, 2), (2, 0, 0), (2, 0, 3), (1, 2, 1), (2, 3, 0)),
    ((0, 0, 1), (3, 0, 1), (3, 0, 3), (2, 0, 2), (2, 0, 1), (3, 3, 3), (2, 1, 1), (3, 2, 0)),
    ((0, 0, 2), (0, 1, 1), (0, 1, 0), (0, 1, 2), (3, 1, 3), (1, 1, 3), (3, 1, 2), (3, 2, 2)),
    ((0, 0, 3), (0, 3, 3), (0, 3, 1), (0, 3, 0), (0, 2, 0), (3, 3, 2), (1, 3, 2), (1, 2, 3)),
)
LAG = 6
CUT = 2
CHUNK = 128 // CUT
CHUNKS = 42 * CUT
FIRST = 28 * CUT
T_SLOTS = CHUNKS + 3 * LAG
T_STEPS = CHUNKS + 4 * LAG
STAGE = LAG + 1
RING = 5 * LAG + 1


def relay_tables():
    relay, arrive = {}, [{} for _ in TREES]
    for tree, edges in enumerate(TREES):
        came = {(0, 0): (None, 0)}
        for x, y, link in edges:
            via, depth = came[(x, y)]
            to = ((x + STEP_XY[link][0]) % 4, (y + STEP_XY[link][1]) % 4)
            came[to] = (link, depth + 1)
            relay.setdefault((link, link ^ 1 if via is None else via), []).append(y * 4 + x)
            if to in OWNERS:
                arrive[tree].setdefault((link, LAG * depth), []).append(to[1] * 4 + to[0])
    return relay, arrive


OWNERS = ((1, 0), (1, 1), (3, 0), (3, 3), (0, 2))
RELAY, ARRIVE = relay_tables()
MASKS = [("relay", key) for key in sorted(RELAY)] + [
    ("arrive", tree, key) for tree in range(4) for key in sorted(ARRIVE[tree])
]
MASK_AT = {name: i for i, name in enumerate(MASKS)}


def rcopy(src, dst, ssem, rsem, dev):
    return pltpu.make_async_remote_copy(
        src_ref=src,
        dst_ref=dst,
        send_sem=ssem,
        recv_sem=rsem,
        device_id=dev,
        device_id_type=pl.DeviceIdType.MESH,
    )


def lanes(start, size):
    return pl.ds(pl.multiple_of(start, 128), size)


def rows16(start, size):
    return pl.ds(pl.multiple_of(start, 16), size)


def layer_kernel(
    req, routes, gates, replica, placement, copy_plan, capacity, gate, up, down, out,
    xs, meta, xin, xmeta, outg, tgo, tgi, rows, hw, hot, rb, sb, mk, acc, hid, part, sibr, zs, za, zb, rp, rm,
    eo, ret, wc, outb, fin,
    load_sem, x_ss, x_rs, m_ss, m_rs, a_ss, a_rs, t_ss, t_rs,
    b_ss, b_rs, gz_ss, gz_rs, gs_ss, gs_rs, s_ss, s_rs, z_ss, z_rs, r_ss, r_rs, f_ss, f_rs,
):
    e = lax.axis_index("ep")
    w = lax.axis_index("wide")
    ex, ey = e % 4, e // 4
    z, c = w // 2, w % 2

    def wide_dev(other):
        return {"ep": e, "wide": other}

    def ep_dev(other):
        return {"ep": other, "wide": w}

    def z_dev(shift):
        return wide_dev(((z + shift) % 4) * 2 + c)

    sibling = wide_dev(z * 2 + 1 - c)
    link_dev = [
        ep_dev(((ey + dy + 4) % 4) * 4 + (ex + dx + 4) % 4) for dx, dy in STEP_XY
    ]

    def load_weights(j, carry):
        for i, ref in enumerate((gate, up)):
            pltpu.make_async_copy(ref.at[:, j], hw.at[pl.ds(56 * i + TILES * j, TILES)], load_sem).start()
        return carry

    lax.fori_loop(0, NW, load_weights, 0)

    def load_down(j, carry):
        for half in range(2):
            pltpu.make_async_copy(
                down.at[pl.ds(half * 128, 128), lanes(j * 256, 256)], hw.at[112 + 2 * j + half], load_sem
            ).start()
        return carry

    lax.fori_loop(0, 28, load_down, 0)

    barrier = pltpu.get_barrier_semaphore()
    for j in range(1, NW):
        pl.semaphore_signal(barrier, inc=1, device_id=wide_dev((w + j) % NW), device_id_type=pl.DeviceIdType.MESH)
    for j in range(1, NE):
        pl.semaphore_signal(barrier, inc=1, device_id=ep_dev((e + j) % NE), device_id_type=pl.DeviceIdType.MESH)

    both = jnp.concatenate([req[0].astype(F32), req[1].astype(F32)], axis=0).astype(BF)
    for k in range(NW):
        for q in range(TILES):
            xs[k, :, q * 128 : (q + 1) * 128] = both[:, q * 1024 + k * 128 : q * 1024 + (k + 1) * 128]
    lane8 = lax.broadcasted_iota(jnp.int32, (8, 128), 1)
    for s in range(STEPS):
        line = jnp.zeros((8, 128), F32)
        for i, ref in enumerate((routes[s], replica[...], gates[s])):
            values = ref.astype(F32).T
            for k in range(2):
                line = jnp.where(lane8 == 2 * i + k, jnp.broadcast_to(values[:, k : k + 1], (8, 128)), line)
        meta[s * 8 : (s + 1) * 8, :] = line

    def spread_row(values):
        line = jnp.zeros((8, 128), jnp.int32)
        for i, value in enumerate(values):
            line = jnp.where(lane8 == i, value, line)
        return jnp.broadcast_to(line[0:1, :].astype(F32), (128, 128))

    home = placement[copy_plan[0]]
    place = ((ey - home // 4 + 4) % 4) * 4 + (ex - home % 4 + 4) % 4
    places = jnp.full((16, 256), place, jnp.int32)
    for i, name in enumerate(MASKS):
        mask = jnp.zeros((16, 256), F32)
        for at in RELAY[name[1]] if name[0] == "relay" else ARRIVE[name[1]][name[2]]:
            mask = jnp.where(places == at, 1.0, mask)
        mk[i] = mask.astype(BF)

    pl.semaphore_wait(barrier, NW - 1 + NE - 1)

    def exchange(j, peer, at):
        return (
            rcopy(xs.at[(w + j) % NW], xin.at[at], x_ss.at[j - 1], x_rs.at[j - 1], wide_dev(peer)),
            rcopy(meta, xmeta.at[at], m_ss.at[j - 1], m_rs.at[j - 1], wide_dev(peer)),
        )

    for j in range(1, NW):
        for copy in reversed(exchange(j, (w + j) % NW, w)):
            copy.start()
    xin[w] = xs[w]
    xmeta[w] = meta[...]
    pltpu.make_async_copy(hw, hw, load_sem).wait()

    def slot_copy(link, t):
        return rcopy(
            sb.at[link, t % STAGE], rb.at[link, t % RING], b_ss.at[link, t % STAGE], b_rs.at[link, t % RING],
            link_dev[link],
        )

    def chunk_of(ref, tree, n, later):
        block = n // CUT
        if later:
            block -= FIRST // CUT
            block = 112 + (block // 2 * 4 + tree) * 2 + block % 2
        else:
            block += tree * (FIRST // CUT)
        return ref.at[block, rows16(n % CUT * CHUNK, CHUNK)]

    def masked(block, mask):
        return block.reshape(CHUNK // 16, 16, 256) * mk[MASK_AT[mask]][None]

    def add(total, term):
        return term if total is None else total + term

    def step(t, own, own_later, recv, wait, send, deliver, deliver_later):
        if recv:
            for link in range(4):
                slot_copy(link, t - LAG).wait_recv()
        if send:
            for link in range(4):
                if wait:
                    slot_copy(link, t - STAGE).wait_send()
                total = None
                for k in range(4):
                    if (link, k) not in RELAY:
                        continue
                    if k == link ^ 1:
                        if own:
                            total = add(total, masked(chunk_of(hw, link, t, own_later)[...], ("relay", (link, k))))
                    elif recv:
                        total = add(total, masked(rb[k, (t - LAG) % RING], ("relay", (link, k))))
                sb[link, t % STAGE] = total.reshape(CHUNK, 256)
                slot_copy(link, t).start()
        if deliver:
            n = t - 4 * LAG
            for tree in range(4):
                total = None
                for link, behind in sorted(ARRIVE[tree]):
                    block = rb[link, (n + behind) % RING]
                    total = add(total, masked(block, ("arrive", tree, (link, behind))))
                chunk_of(hot, tree, n, deliver_later)[...] = total.reshape(CHUNK, 256)

    cursor = [0]

    def run_to(t1):
        t0 = cursor[0]
        t1 = max(t0, min(T_STEPS, t1))
        cursor[0] = t1
        marks = (LAG, STAGE, FIRST, CHUNKS, T_SLOTS, 4 * LAG, 4 * LAG + FIRST)
        cuts = sorted({t0, t1, *[x for x in marks if t0 < x < t1]})
        for lo, hi in zip(cuts[:-1], cuts[1:]):
            kind = (
                lo < CHUNKS, lo >= FIRST, lo >= LAG, lo >= STAGE, lo < T_SLOTS, lo >= 4 * LAG, lo >= 4 * LAG + FIRST
            )
            if hi - lo == 1:
                step(lo, *kind)
            else:
                def body(t, carry, kind=kind):
                    step(t, *kind)
                    return carry

                lax.fori_loop(lo, hi, body, 0)

    def run(count):
        run_to(cursor[0] + count * CUT)

    def drain_slots():
        def drain_send(t, carry):
            for link in range(4):
                slot_copy(link, t).wait_send()
            return carry

        lax.fori_loop(T_SLOTS - STAGE, T_SLOTS, drain_send, 0)

    def make_plan():
        picks = xmeta[...].reshape(128, 128)
        lane = lax.broadcasted_iota(jnp.int32, (128, 128), 1)
        line = lax.broadcasted_iota(jnp.int32, (128, 128), 0)
        lane_f = lane.astype(F32)
        second = (line // 8) % 2 == 1
        limits = jnp.where(
            second,
            spread_row([capacity[1, i] for i in range(NE)]),
            spread_row([capacity[0, i] for i in range(NE)]),
        )
        slot_of = spread_row([placement[i] for i in range(NE)])
        cand = spread_row([home] + [(home + copy_plan[i]) % NE for i in range(1, 4)])
        hot_id = jnp.full((128, 128), copy_plan[0], jnp.int32).astype(F32)
        zero = jnp.zeros((128, 128), F32)

        def spread(column):
            return jnp.broadcast_to(picks[:, column : column + 1], (128, 128))

        def total(v):
            return jnp.broadcast_to(jnp.sum(v, axis=1, keepdims=True), (128, 128))

        onehots, servers, copied = [], [], []
        for k in range(2):
            route, pick = spread(k), spread(2 + k)
            server = total(jnp.where(lane_f == route, slot_of, zero))
            chosen = total(jnp.where(lane_f == pick, cand, zero))
            is_hot = jnp.where(second, jnp.where(route == hot_id, 1.0, 0.0), 0.0)
            server = jnp.where(is_hot > 0.5, chosen, server)
            copied.append(jnp.where(pick > 0.5, is_hot, 0.0))
            servers.append(server)
            onehots.append(jnp.where(lane_f == server, 1.0, 0.0))
        earlier = jnp.where(lane < line, 1.0, 0.0) * jnp.where((line // 8) % 2 == (lane // 8) % 2, 1.0, 0.0)
        before = jnp.dot(earlier.astype(BF), (onehots[0] + onehots[1]).astype(BF), preferred_element_type=F32)
        lane_w = lax.broadcasted_iota(jnp.int32, (128, 512), 1).astype(F32)
        base = jnp.where(second, float(SLOTS), 0.0)
        matches = []
        for k in range(2):
            count = before if k == 0 else before + onehots[0]
            position = total(count * onehots[k])
            limit = total(limits * onehots[k])
            column = jnp.where(position < limit, base + servers[k] * CAP + position, -1.0)
            matches.append(jnp.where(lane_w == jnp.broadcast_to(column[:, :1], (128, 512)), 1.0, 0.0))

        def wide512(v):
            return jnp.broadcast_to(v[:, :1], (128, 512))

        wc[...] = (matches[0] * wide512(spread(4)) + matches[1] * wide512(spread(5))).astype(BF)
        dispatch = (matches[0] + matches[1]).astype(BF)
        tags = (matches[0] * wide512(copied[0]) + matches[1] * wide512(copied[1])).astype(BF)
        flat = xin[...].reshape(128, COLS)
        contract = (((0,), (0,)), ((), ()))
        for s in range(STEPS):
            outg[s] = lax.dot_general(
                dispatch[:, s * SLOTS : (s + 1) * SLOTS], flat, contract, preferred_element_type=F32
            ).astype(BF)
        tgo[...] = lax.dot_general(
            tags[:, SLOTS:], jnp.ones((128, 128), BF), contract, preferred_element_type=F32
        ).astype(BF)

    def a2a_start(s):
        def send(j, carry):
            peer = (e + j) % NE
            rcopy(
                outg.at[s, rows16(peer * CAP, CAP)], rows.at[s, rows16(e * CAP, CAP), lanes(w * COLS, COLS)],
                a_ss.at[s], a_rs.at[s], ep_dev(peer),
            ).start()
            if s == 1:
                rcopy(
                    tgo.at[rows16(peer * CAP, CAP)], tgi.at[rows16(e * CAP, CAP)], t_ss, t_rs, ep_dev(peer)
                ).start()
            return carry

        lax.fori_loop(1, NE, send, 0)
        rows[s, rows16(e * CAP, CAP), lanes(w * COLS, COLS)] = outg[s, rows16(e * CAP, CAP), :]
        if s == 1:
            tgi[rows16(e * CAP, CAP), :] = tgo[rows16(e * CAP, CAP), :]

    def a2a_wait(s):
        n = (NE - 1) * CAP
        done = rcopy(
            outg.at[s, pl.ds(0, n)], rows.at[s, pl.ds(0, n), lanes(w * COLS, COLS)], a_ss.at[s], a_rs.at[s],
            ep_dev((e + 1) % NE),
        )
        done.wait_recv()
        done.wait_send()
        if s == 1:
            done = rcopy(tgo.at[pl.ds(0, n)], tgi.at[pl.ds(0, n)], t_ss, t_rs, ep_dev((e + 1) % NE))
            done.wait_recv()
            done.wait_send()

    def shard(s, shift, core, half):
        col = (((z + shift + 4) % 4) * 2 + core) * COLS
        lo, n = (0, SLOTS) if half is None else (half * HALF, HALF)
        return rows.at[s, pl.ds(lo, n), lanes(col, COLS)]

    GZ = ((1, 0, 0), (1, 0, 1), (-1, 0, 1), (-1, 0, 0), (1, -1, 0), (-1, 1, 1))

    def gz_send(s, k):
        direction, shift, half = GZ[k]
        src = shard(s, shift, c, half)
        return rcopy(src, src, gz_ss.at[s, k], gz_rs.at[s, k], z_dev(direction + 4))

    def gz_wait(s, k):
        direction, shift, half = GZ[k]
        ref = shard(s, shift - direction, c, half)
        rcopy(ref, ref, gz_ss.at[s, k], gz_rs.at[s, k], z_dev(direction + 4)).wait_recv()

    GS = ((0, None), (-1, 0), (1, 1), (-1, 1), (1, 0), (2, 0), (2, 1))

    def gs_send(s, k):
        src = shard(s, GS[k][0], c, GS[k][1])
        return rcopy(src, src, gs_ss.at[s, k], gs_rs.at[s, k], sibling)

    def gs_wait(s, k):
        ref = shard(s, GS[k][0], 1 - c, GS[k][1])
        rcopy(ref, ref, gs_ss.at[s, k], gs_rs.at[s, k], sibling).wait_recv()

    def gather0(s):
        for k in (0, 2, 1, 3):
            gz_send(s, k).start()
        gs_send(s, 0).start()

    def gather1(s):
        gz_wait(s, 0)
        gz_send(s, 4).start()
        gs_send(s, 1).start()
        gz_wait(s, 2)
        gz_send(s, 5).start()
        gs_send(s, 2).start()

    def gather2(s):
        gz_wait(s, 1)
        gs_send(s, 3).start()
        gz_wait(s, 3)
        gs_send(s, 4).start()

    def gather3(s):
        gz_wait(s, 4)
        gs_send(s, 5).start()
        gz_wait(s, 5)
        gs_send(s, 6).start()

    def gather4(s):
        for k in range(7):
            gs_wait(s, k)

    def gather_drain(s):
        for k in range(6):
            gz_send(s, k).wait_send()
        for k in range(7):
            gs_send(s, k).wait_send()

    def hidden(s, weights, slots):
        for k in range(4):
            x = rows[s, :, k * 1792 : (k + 1) * 1792]
            for i in range(2):
                v = jnp.dot(
                    x, weights[56 * i + 14 * k : 56 * i + 14 * k + 14].reshape(1792, 256), preferred_element_type=F32
                )
                acc[i] = v if k == 0 else acc[i] + v
            run(slots)
        g = acc[0]
        return g / (1.0 + jnp.exp(-g)) * acc[1]

    def copy_tag():
        tag = tgi[...].astype(F32)
        return jnp.concatenate([tag, tag], axis=1)

    PARTS = ((0, 0, TILES), (1, 0, 2), (1, 2, 2), (1, 4, 2), (1, 6, 1))

    def own_cols(p):
        return pl.ds(PARTS[p][1] * 128, PARTS[p][2] * 128)

    def block_cols(p, zi, core):
        return lanes((((z + zi) % 4) * 2 + core) * COLS + PARTS[p][1] * 128, PARTS[p][2] * 128)

    def sib_copy(p, zi):
        s = PARTS[p][0]
        return rcopy(
            part.at[s, :, block_cols(p, zi, 1 - c)], sibr.at[s, zi, :, own_cols(p)],
            s_ss.at[p, zi], s_rs.at[p, zi], sibling,
        )

    def partials(p, slots):
        s, first, count = PARTS[p]
        for zi in (2, 1, 3, 0):
            zz = (z + zi) % 4
            for q in range(first, first + count):
                at = pl.ds(112 + 2 * (q * 4 + zz), 2)
                v = jnp.dot(hid[s], hw[at].reshape(256, 256), preferred_element_type=F32)
                if s == 1:
                    v += jnp.dot(hid[2], hot[at].reshape(256, 256), preferred_element_type=F32)
                v = v.astype(BF)
                for core in range(2):
                    part[s, :, lanes((zz * 2 + core) * COLS + q * 128, 128)] = v[:, core * 128 : (core + 1) * 128]
            sib_copy(p, zi).start()
            run(slots)

    def pair_sum(p, zi):
        s = PARTS[p][0]
        return part[s, :, block_cols(p, zi, c)].astype(F32) + sibr[s, zi, :, own_cols(p)].astype(F32)

    lo_half, hi_half = pl.ds(0, HALF), pl.ds(HALF, HALF)

    def z_copy(p, k):
        s, cols = PARTS[p][0], own_cols(p)
        src, dst, direction = (
            (zs.at[s, 0, lo_half, cols], za.at[s, :, cols], 1),
            (zs.at[s, 0, hi_half, cols], zb.at[s, :, cols], -1),
            (zs.at[s, 1, hi_half, cols], rp.at[s, hi_half, cols], 1),
            (zs.at[s, 1, lo_half, cols], rp.at[s, lo_half, cols], 1),
            (zs.at[s, 2, lo_half, cols], rm.at[s, lo_half, cols], -1),
            (zs.at[s, 2, hi_half, cols], rm.at[s, hi_half, cols], -1),
        )[k]
        return rcopy(src, dst, z_ss.at[p, k], z_rs.at[p, k], z_dev(direction + 4))

    def reduce1(p):
        s, cols = PARTS[p][0], own_cols(p)
        sib_copy(p, 2).wait_recv()
        zs[s, 0, :, cols] = pair_sum(p, 2).astype(BF)
        z_copy(p, 0).start()
        z_copy(p, 1).start()
        sib_copy(p, 1).wait_recv()
        zs[s, 1, :, cols] = pair_sum(p, 1).astype(BF)
        z_copy(p, 2).start()
        sib_copy(p, 3).wait_recv()
        zs[s, 2, :, cols] = pair_sum(p, 3).astype(BF)
        z_copy(p, 4).start()

    def reduce2(p):
        s, cols = PARTS[p][0], own_cols(p)
        z_copy(p, 0).wait_recv()
        zs[s, 1, lo_half, cols] = (zs[s, 1, lo_half, cols].astype(F32) + za[s, :, cols].astype(F32)).astype(BF)
        z_copy(p, 3).start()
        z_copy(p, 1).wait_recv()
        zs[s, 2, hi_half, cols] = (zs[s, 2, hi_half, cols].astype(F32) + zb[s, :, cols].astype(F32)).astype(BF)
        z_copy(p, 5).start()

    def reduce3(p):
        s, cols = PARTS[p][0], own_cols(p)
        sib_copy(p, 0).wait_recv()
        for k in (2, 4, 3, 5):
            z_copy(p, k).wait_recv()
        eo[s, :, cols] = (pair_sum(p, 0) + rp[s, :, cols].astype(F32) + rm[s, :, cols].astype(F32)).astype(BF)

    def reduce_drain(p):
        for zi in range(4):
            sib_copy(p, zi).wait_send()
        for k in range(6):
            z_copy(p, k).wait_send()

    def back_start(p):
        s, cols = PARTS[p][0], own_cols(p)

        def send(j, carry):
            peer = (e + j) % NE
            rcopy(
                eo.at[s, rows16(peer * CAP, CAP), cols], ret.at[rows16(s * SLOTS + e * CAP, CAP), cols],
                r_ss.at[p], r_rs.at[p], ep_dev(peer),
            ).start()
            return carry

        lax.fori_loop(1, NE, send, 0)
        ret[rows16(s * SLOTS + e * CAP, CAP), cols] = eo[s, rows16(e * CAP, CAP), cols]

    def back_wait(p):
        s, cols = PARTS[p][0], own_cols(p)
        n = (NE - 1) * CAP
        done = rcopy(
            eo.at[s, pl.ds(0, n), cols], ret.at[pl.ds(s * SLOTS, n), cols], r_ss.at[p], r_rs.at[p],
            ep_dev((e + 1) % NE),
        )
        done.wait_recv()
        done.wait_send()

    def final(p, j, at):
        peer = (w + j) % NW
        cols = own_cols(p)
        return rcopy(
            outb.at[rows16(peer * 16, 16), cols], fin.at[at, :, cols], f_ss.at[p - 1, j - 1], f_rs.at[p - 1, j - 1],
            wide_dev(peer),
        )

    def combine(p):
        cols = own_cols(p)
        outb[:, cols] = jnp.dot(wc[...], ret[:, cols], preferred_element_type=F32).astype(BF)
        for j in range(1, NW):
            final(p, j, w).start()
        fin[w, :, cols] = outb[rows16(w * 16, 16), cols]

    run(5)
    for j in range(1, NW):
        for copy in exchange(j, (w + j) % NW, (w + NW - j) % NW):
            copy.wait_recv()
    make_plan()
    a2a_start(0)
    run_to(8 * CUT)
    a2a_wait(0)
    gather0(0)
    a2a_start(1)
    run_to(12 * CUT)
    gather1(0)
    a2a_wait(1)
    run_to(16 * CUT)
    gather2(0)
    gather0(1)
    run_to(19 * CUT)
    gather3(0)
    run_to(20 * CUT)
    gather4(0)
    hid[0] = hidden(0, hw, 1).astype(BF)
    gather1(1)
    partials(0, 1)
    gather2(1)
    reduce1(0)
    run_to(31 * CUT)
    gather3(1)
    run_to(32 * CUT)
    gather4(1)
    hid[1] = (hidden(1, hw, 1) * (1.0 - copy_tag())).astype(BF)
    reduce2(0)
    run_to(4 * LAG + FIRST)
    hid[2] = (hidden(1, hot, 1) * copy_tag()).astype(BF)
    reduce3(0)
    run_to(4 * LAG + FIRST + 4 * CUT)
    partials(1, 0)
    run(2)
    reduce1(1)
    run_to(4 * LAG + FIRST + 8 * CUT)
    partials(2, 0)
    reduce2(1)
    run(1)
    reduce1(2)
    run_to(4 * LAG + FIRST + 12 * CUT)
    partials(3, 0)
    reduce2(2)
    run(1)
    reduce1(3)
    run(T_STEPS)
    partials(4, 0)
    reduce3(1)
    back_start(1)
    reduce2(3)
    reduce1(4)
    back_start(0)
    reduce3(2)
    back_start(2)
    reduce2(4)
    reduce3(3)
    back_start(3)
    reduce3(4)
    back_start(4)
    back_wait(0)
    back_wait(1)
    combine(1)
    back_wait(2)
    combine(2)
    back_wait(3)
    combine(3)
    drain_slots()
    for j in range(1, NW):
        for copy in exchange(j, (w + j) % NW, w):
            copy.wait_send()
    for s in range(STEPS):
        gather_drain(s)
    for p in range(5):
        reduce_drain(p)
    back_wait(4)
    combine(4)
    for p in (1, 2, 3, 4):
        for j in range(1, NW):
            final(p, j, (w + NW - j) % NW).wait_recv()
    blocks = [fin[k].astype(F32) for k in range(NW)]
    for q in range(TILES):
        line = jnp.concatenate([block[:, q * 128 : (q + 1) * 128] for block in blocks], axis=1)
        for s in range(STEPS):
            out[s, :, q * 1024 : (q + 1) * 1024] = line[s * 8 : (s + 1) * 8].astype(BF)
    for p in (1, 2, 3, 4):
        for j in range(1, NW):
            final(p, j, w).wait_send()


def shards(
    requests, routes, gates, replica, placement, copy_plan, capacity, gate_proj, up_proj, down_proj
):
    vmem = pl.BlockSpec(memory_space=pltpu.VMEM)
    smem = pl.BlockSpec(memory_space=pltpu.SMEM)
    hbm = pl.BlockSpec(memory_space=pl.ANY)
    dma = pltpu.SemaphoreType.DMA
    return pl.pallas_call(
        layer_kernel,
        out_shape=jax.ShapeDtypeStruct(requests.shape, BF),
        in_specs=[vmem, vmem, vmem, vmem, smem, smem, smem, hbm, hbm, hbm],
        out_specs=vmem,
        scratch_shapes=[
            pltpu.VMEM((NW, 16, COLS), BF),
            pltpu.VMEM((16, 128), F32),
            pltpu.VMEM((NW, 16, COLS), BF),
            pltpu.VMEM((NW, 16, 128), F32),
            pltpu.VMEM((STEPS, SLOTS, COLS), BF),
            pltpu.VMEM((SLOTS, 128), BF),
            pltpu.VMEM((SLOTS, 128), BF),
            pltpu.VMEM((STEPS, SLOTS, D), BF),
            pltpu.VMEM((168, 128, 256), BF),
            pltpu.VMEM((168, 128, 256), BF),
            pltpu.VMEM((4, RING, CHUNK, 256), BF),
            pltpu.VMEM((4, STAGE, CHUNK, 256), BF),
            pltpu.VMEM((len(MASKS), 16, 256), BF),
            pltpu.VMEM((2, SLOTS, HID), F32),
            pltpu.VMEM((3, SLOTS, HID), BF),
            pltpu.VMEM((STEPS, SLOTS, D), BF),
            pltpu.VMEM((STEPS, 4, SLOTS, COLS), BF),
            pltpu.VMEM((STEPS, 3, SLOTS, COLS), BF),
            pltpu.VMEM((STEPS, HALF, COLS), BF),
            pltpu.VMEM((STEPS, HALF, COLS), BF),
            pltpu.VMEM((STEPS, SLOTS, COLS), BF),
            pltpu.VMEM((STEPS, SLOTS, COLS), BF),
            pltpu.VMEM((STEPS, SLOTS, COLS), BF),
            pltpu.VMEM((STEPS * SLOTS, COLS), BF),
            pltpu.VMEM((128, STEPS * SLOTS), BF),
            pltpu.VMEM((128, COLS), BF),
            pltpu.VMEM((NW, 16, COLS), BF),
            dma,
            dma((7,)), dma((7,)), dma((7,)), dma((7,)),
            dma((2,)), dma((2,)), dma, dma,
            dma((4, STAGE)), dma((4, RING)),
            dma((2, 6)), dma((2, 6)), dma((2, 7)), dma((2, 7)),
            dma((5, 4)), dma((5, 4)), dma((5, 6)), dma((5, 6)),
            dma((5,)), dma((5,)), dma((4, 7)), dma((4, 7)),
        ],
        compiler_params=pltpu.CompilerParams(
            collective_id=0, has_side_effects=True, vmem_limit_bytes=62 * 1024 * 1024
        ),
        name="expert_layer",
    )(
        requests, jnp.swapaxes(routes, 1, 2), jnp.swapaxes(gates, 1, 2), replica.T, placement, copy_plan, capacity,
        gate_proj.reshape(TILES, NW, 128, HID), up_proj.reshape(TILES, NW, 128, HID), down_proj.reshape(HID, D),
    )


def solution(mesh):
    rows = P(None, ("ep", "wide"), None)
    placed = (
        rows, rows, rows, P(("ep", "wide"), None), P(), P(), P(),
        P("ep", None, "wide"), P("ep", None, "wide"), P("ep", "wide", None),
    )
    return jax.shard_map(shards, mesh=mesh, in_specs=placed, out_specs=rows, check_vma=False)
```

```python
import jax
import jax.numpy as jnp
from jax import lax
from jax.experimental import pallas as pl
from jax.experimental.pallas import tpu as pltpu
from jax.sharding import PartitionSpec as P

BF = jnp.bfloat16
F32 = jnp.float32
STEPS = 2
CAP = 16
NE = 16
NW = 8
GROUP = 64
D = 7168
COLS = D // NW
SLOTS = NE * CAP
HALF = SLOTS // 2
HID = 256

TILES = COLS // 128

STEP_XY = ((1, 0), (-1, 0), (0, 1), (0, -1))
TREES = (
    ((0, 0, 0), (1, 0, 2), (1, 0, 0), (1, 1, 2), (2, 0, 0), (2, 0, 3), (1, 2, 1), (2, 3, 0)),
    ((0, 0, 1), (3, 0, 1), (3, 0, 3), (2, 0, 2), (2, 0, 1), (3, 3, 3), (2, 1, 1), (3, 2, 0)),
    ((0, 0, 2), (0, 1, 1), (0, 1, 0), (0, 1, 2), (3, 1, 3), (1, 1, 3), (3, 1, 2), (3, 2, 2)),
    ((0, 0, 3), (0, 3, 3), (0, 3, 1), (0, 3, 0), (0, 2, 0), (3, 3, 2), (1, 3, 2), (1, 2, 3)),
)
LAG = 6
CUT = 2
CHUNK = 128 // CUT
CHUNKS = 42 * CUT
FIRST = 28 * CUT
T_SLOTS = CHUNKS + 3 * LAG
T_STEPS = CHUNKS + 4 * LAG
STAGE = LAG + 1
RING = 5 * LAG + 1


def relay_tables():
    relay, arrive = {}, [{} for _ in TREES]
    for tree, edges in enumerate(TREES):
        came = {(0, 0): (None, 0)}
        for x, y, link in edges:
            via, depth = came[(x, y)]
            to = ((x + STEP_XY[link][0]) % 4, (y + STEP_XY[link][1]) % 4)
            came[to] = (link, depth + 1)
            relay.setdefault((link, link ^ 1 if via is None else via), []).append(y * 4 + x)
            if to in OWNERS:
                arrive[tree].setdefault((link, LAG * depth), []).append(to[1] * 4 + to[0])
    return relay, arrive


OWNERS = ((1, 0), (1, 1), (3, 0), (3, 3), (0, 2))
RELAY, ARRIVE = relay_tables()
MASKS = [("relay", key) for key in sorted(RELAY)] + [
    ("arrive", tree, key) for tree in range(4) for key in sorted(ARRIVE[tree])
]
MASK_AT = {name: i for i, name in enumerate(MASKS)}


def rcopy(src, dst, ssem, rsem, dev):
    return pltpu.make_async_remote_copy(
        src_ref=src,
        dst_ref=dst,
        send_sem=ssem,
        recv_sem=rsem,
        device_id=dev,
        device_id_type=pl.DeviceIdType.MESH,
    )


def lanes(start, size):
    return pl.ds(pl.multiple_of(start, 128), size)


def rows16(start, size):
    return pl.ds(pl.multiple_of(start, 16), size)


def layer_kernel(
    req, routes, gates, replica, placement, copy_plan, capacity, gate, up, down, out,
    xs, meta, xin, xmeta, outg, tgo, tgi, rows, hw, hot, rb, sb, mk, acc, hid, part, sibr, zs, za, zb, rp, rm,
    eo, ret, wc, outb, fin,
    load_sem, x_ss, x_rs, m_ss, m_rs, a_ss, a_rs, t_ss, t_rs,
    b_ss, b_rs, gz_ss, gz_rs, gs_ss, gs_rs, s_ss, s_rs, z_ss, z_rs, r_ss, r_rs, f_ss, f_rs,
):
    e = lax.axis_index("ep")
    w = lax.axis_index("wide")
    ex, ey = e % 4, e // 4
    z, c = w // 2, w % 2

    def wide_dev(other):
        return {"ep": e, "wide": other}

    def ep_dev(other):
        return {"ep": other, "wide": w}

    def z_dev(shift):
        return wide_dev(((z + shift) % 4) * 2 + c)

    sibling = wide_dev(z * 2 + 1 - c)
    link_dev = [
        ep_dev(((ey + dy + 4) % 4) * 4 + (ex + dx + 4) % 4) for dx, dy in STEP_XY
    ]

    def load_weights(j, carry):
        for i, ref in enumerate((gate, up)):
            pltpu.make_async_copy(ref.at[:, j], hw.at[pl.ds(56 * i + TILES * j, TILES)], load_sem).start()
        return carry

    lax.fori_loop(0, NW, load_weights, 0)

    def load_down(j, carry):
        for half in range(2):
            pltpu.make_async_copy(
                down.at[pl.ds(half * 128, 128), lanes(j * 256, 256)], hw.at[112 + 2 * j + half], load_sem
            ).start()
        return carry

    lax.fori_loop(0, 28, load_down, 0)

    barrier = pltpu.get_barrier_semaphore()
    for j in range(1, NW):
        pl.semaphore_signal(barrier, inc=1, device_id=wide_dev((w + j) % NW), device_id_type=pl.DeviceIdType.MESH)
    for j in range(1, NE):
        pl.semaphore_signal(barrier, inc=1, device_id=ep_dev((e + j) % NE), device_id_type=pl.DeviceIdType.MESH)

    both = jnp.concatenate([req[0].astype(F32), req[1].astype(F32)], axis=0).astype(BF)
    for k in range(NW):
        for q in range(TILES):
            xs[k, :, q * 128 : (q + 1) * 128] = both[:, q * 1024 + k * 128 : q * 1024 + (k + 1) * 128]
    lane8 = lax.broadcasted_iota(jnp.int32, (8, 128), 1)
    for s in range(STEPS):
        line = jnp.zeros((8, 128), F32)
        for i, ref in enumerate((routes[s], replica[...], gates[s])):
            values = ref.astype(F32).T
            for k in range(2):
                line = jnp.where(lane8 == 2 * i + k, jnp.broadcast_to(values[:, k : k + 1], (8, 128)), line)
        meta[s * 8 : (s + 1) * 8, :] = line

    def spread_row(values):
        line = jnp.zeros((8, 128), jnp.int32)
        for i, value in enumerate(values):
            line = jnp.where(lane8 == i, value, line)
        return jnp.broadcast_to(line[0:1, :].astype(F32), (128, 128))

    home = placement[copy_plan[0]]
    place = ((ey - home // 4 + 4) % 4) * 4 + (ex - home % 4 + 4) % 4
    places = jnp.full((16, 256), place, jnp.int32)
    for i, name in enumerate(MASKS):
        mask = jnp.zeros((16, 256), F32)
        for at in RELAY[name[1]] if name[0] == "relay" else ARRIVE[name[1]][name[2]]:
            mask = jnp.where(places == at, 1.0, mask)
        mk[i] = mask.astype(BF)

    pl.semaphore_wait(barrier, NW - 1 + NE - 1)

    def exchange(j, peer, at):
        return (
            rcopy(xs.at[(w + j) % NW], xin.at[at], x_ss, x_rs, wide_dev(peer)),
            rcopy(meta, xmeta.at[at], m_ss, m_rs, wide_dev(peer)),
        )

    for j in range(1, NW):
        for copy in reversed(exchange(j, (w + j) % NW, w)):
            copy.start()
    xin[w] = xs[w]
    xmeta[w] = meta[...]
    pltpu.make_async_copy(hw, hw, load_sem).wait()

    def slot_copy(link, t):
        return rcopy(
            sb.at[link, t % STAGE], rb.at[link, t % RING], b_ss.at[link, t % STAGE], b_rs.at[link, t % RING],
            link_dev[link],
        )

    def chunk_of(ref, tree, n, later):
        block = n // CUT
        if later:
            block -= FIRST // CUT
            block = 112 + (block // 2 * 4 + tree) * 2 + block % 2
        else:
            block += tree * (FIRST // CUT)
        return ref.at[block, rows16(n % CUT * CHUNK, CHUNK)]

    def masked(block, mask):
        return block.reshape(CHUNK // 16, 16, 256) * mk[MASK_AT[mask]][None]

    def add(total, term):
        return term if total is None else total + term

    def step(t, own, own_later, recv, wait, send, deliver, deliver_later):
        if recv:
            for link in range(4):
                slot_copy(link, t - LAG).wait_recv()
        if send:
            for link in range(4):
                if wait:
                    slot_copy(link, t - STAGE).wait_send()
                total = None
                for k in range(4):
                    if (link, k) not in RELAY:
                        continue
                    if k == link ^ 1:
                        if own:
                            total = add(total, masked(chunk_of(hw, link, t, own_later)[...], ("relay", (link, k))))
                    elif recv:
                        total = add(total, masked(rb[k, (t - LAG) % RING], ("relay", (link, k))))
                sb[link, t % STAGE] = total.reshape(CHUNK, 256)
                slot_copy(link, t).start()
        if deliver:
            n = t - 4 * LAG
            for tree in range(4):
                total = None
                for link, behind in sorted(ARRIVE[tree]):
                    block = rb[link, (n + behind) % RING]
                    total = add(total, masked(block, ("arrive", tree, (link, behind))))
                chunk_of(hot, tree, n, deliver_later)[...] = total.reshape(CHUNK, 256)

    cursor = [0]

    def run_to(t1):
        t0 = cursor[0]
        t1 = max(t0, min(T_STEPS, t1))
        cursor[0] = t1
        marks = (LAG, STAGE, FIRST, CHUNKS, T_SLOTS, 4 * LAG, 4 * LAG + FIRST)
        cuts = sorted({t0, t1, *[x for x in marks if t0 < x < t1]})
        for lo, hi in zip(cuts[:-1], cuts[1:]):
            kind = (
                lo < CHUNKS, lo >= FIRST, lo >= LAG, lo >= STAGE, lo < T_SLOTS, lo >= 4 * LAG, lo >= 4 * LAG + FIRST
            )
            if hi - lo == 1:
                step(lo, *kind)
            else:
                def body(t, carry, kind=kind):
                    step(t, *kind)
                    return carry

                lax.fori_loop(lo, hi, body, 0)

    def run(count):
        run_to(cursor[0] + count * CUT)

    def drain_slots():
        def drain_send(t, carry):
            for link in range(4):
                slot_copy(link, t).wait_send()
            return carry

        lax.fori_loop(T_SLOTS - STAGE, T_SLOTS, drain_send, 0)

    def make_plan():
        picks = xmeta[...].reshape(128, 128)
        lane = lax.broadcasted_iota(jnp.int32, (128, 128), 1)
        line = lax.broadcasted_iota(jnp.int32, (128, 128), 0)
        lane_f = lane.astype(F32)
        second = (line // 8) % 2 == 1
        limits = jnp.where(
            second,
            spread_row([capacity[1, i] for i in range(NE)]),
            spread_row([capacity[0, i] for i in range(NE)]),
        )
        slot_of = spread_row([placement[i] for i in range(NE)])
        cand = spread_row([home] + [(home + copy_plan[i]) % NE for i in range(1, 4)])
        hot_id = jnp.full((128, 128), copy_plan[0], jnp.int32).astype(F32)
        zero = jnp.zeros((128, 128), F32)

        def spread(column):
            return jnp.broadcast_to(picks[:, column : column + 1], (128, 128))

        def total(v):
            return jnp.broadcast_to(jnp.sum(v, axis=1, keepdims=True), (128, 128))

        onehots, servers, copied = [], [], []
        for k in range(2):
            route, pick = spread(k), spread(2 + k)
            server = total(jnp.where(lane_f == route, slot_of, zero))
            chosen = total(jnp.where(lane_f == pick, cand, zero))
            is_hot = jnp.where(second, jnp.where(route == hot_id, 1.0, 0.0), 0.0)
            server = jnp.where(is_hot > 0.5, chosen, server)
            copied.append(jnp.where(pick > 0.5, is_hot, 0.0))
            servers.append(server)
            onehots.append(jnp.where(lane_f == server, 1.0, 0.0))
        earlier = jnp.where(lane < line, 1.0, 0.0) * jnp.where((line // 8) % 2 == (lane // 8) % 2, 1.0, 0.0)
        before = jnp.dot(earlier.astype(BF), (onehots[0] + onehots[1]).astype(BF), preferred_element_type=F32)
        lane_w = lax.broadcasted_iota(jnp.int32, (128, 512), 1).astype(F32)
        base = jnp.where(second, float(SLOTS), 0.0)
        matches = []
        for k in range(2):
            count = before if k == 0 else before + onehots[0]
            position = total(count * onehots[k])
            limit = total(limits * onehots[k])
            column = jnp.where(position < limit, base + servers[k] * CAP + position, -1.0)
            matches.append(jnp.where(lane_w == jnp.broadcast_to(column[:, :1], (128, 512)), 1.0, 0.0))

        def wide512(v):
            return jnp.broadcast_to(v[:, :1], (128, 512))

        wc[...] = (matches[0] * wide512(spread(4)) + matches[1] * wide512(spread(5))).astype(BF)
        dispatch = (matches[0] + matches[1]).astype(BF)
        tags = (matches[0] * wide512(copied[0]) + matches[1] * wide512(copied[1])).astype(BF)
        flat = xin[...].reshape(128, COLS)
        contract = (((0,), (0,)), ((), ()))
        for s in range(STEPS):
            outg[s] = lax.dot_general(
                dispatch[:, s * SLOTS : (s + 1) * SLOTS], flat, contract, preferred_element_type=F32
            ).astype(BF)
        tgo[...] = lax.dot_general(
            tags[:, SLOTS:], jnp.ones((128, 128), BF), contract, preferred_element_type=F32
        ).astype(BF)

    def a2a_start(s):
        def send(j, carry):
            peer = (e + j) % NE
            rcopy(
                outg.at[s, rows16(peer * CAP, CAP)], rows.at[s, rows16(e * CAP, CAP), lanes(w * COLS, COLS)],
                a_ss.at[s], a_rs.at[s], ep_dev(peer),
            ).start()
            if s == 1:
                rcopy(
                    tgo.at[rows16(peer * CAP, CAP)], tgi.at[rows16(e * CAP, CAP)], t_ss, t_rs, ep_dev(peer)
                ).start()
            return carry

        lax.fori_loop(1, NE, send, 0)
        rows[s, rows16(e * CAP, CAP), lanes(w * COLS, COLS)] = outg[s, rows16(e * CAP, CAP), :]
        if s == 1:
            tgi[rows16(e * CAP, CAP), :] = tgo[rows16(e * CAP, CAP), :]

    def a2a_wait(s):
        n = (NE - 1) * CAP
        done = rcopy(
            outg.at[s, pl.ds(0, n)], rows.at[s, pl.ds(0, n), lanes(w * COLS, COLS)], a_ss.at[s], a_rs.at[s],
            ep_dev((e + 1) % NE),
        )
        done.wait_recv()
        done.wait_send()
        if s == 1:
            done = rcopy(tgo.at[pl.ds(0, n)], tgi.at[pl.ds(0, n)], t_ss, t_rs, ep_dev((e + 1) % NE))
            done.wait_recv()
            done.wait_send()

    def shard(s, shift, core, half):
        col = (((z + shift + 4) % 4) * 2 + core) * COLS
        lo, n = (0, SLOTS) if half is None else (half * HALF, HALF)
        return rows.at[s, pl.ds(lo, n), lanes(col, COLS)]

    GZ = ((1, 0, 0), (1, 0, 1), (-1, 0, 1), (-1, 0, 0), (1, -1, 0), (-1, 1, 1))

    def gz_send(s, k):
        direction, shift, half = GZ[k]
        src = shard(s, shift, c, half)
        return rcopy(src, src, gz_ss.at[s, k], gz_rs.at[s, k], z_dev(direction + 4))

    def gz_wait(s, k):
        direction, shift, half = GZ[k]
        ref = shard(s, shift - direction, c, half)
        rcopy(ref, ref, gz_ss.at[s, k], gz_rs.at[s, k], z_dev(direction + 4)).wait_recv()

    GS = ((0, None), (-1, 0), (1, 1), (-1, 1), (1, 0), (2, 0), (2, 1))

    def gs_send(s, k):
        src = shard(s, GS[k][0], c, GS[k][1])
        return rcopy(src, src, gs_ss.at[s, k], gs_rs.at[s, k], sibling)

    def gs_wait(s, k):
        ref = shard(s, GS[k][0], 1 - c, GS[k][1])
        rcopy(ref, ref, gs_ss.at[s, k], gs_rs.at[s, k], sibling).wait_recv()

    def gather0(s):
        for k in (0, 2, 1, 3):
            gz_send(s, k).start()
        gs_send(s, 0).start()

    def gather1(s):
        gz_wait(s, 0)
        gz_send(s, 4).start()
        gs_send(s, 1).start()
        gz_wait(s, 2)
        gz_send(s, 5).start()
        gs_send(s, 2).start()

    def gather2(s):
        gz_wait(s, 1)
        gs_send(s, 3).start()
        gz_wait(s, 3)
        gs_send(s, 4).start()

    def gather3(s):
        gz_wait(s, 4)
        gs_send(s, 5).start()
        gz_wait(s, 5)
        gs_send(s, 6).start()

    def gather4(s):
        for k in range(7):
            gs_wait(s, k)

    def gather_drain(s):
        for k in range(6):
            gz_send(s, k).wait_send()
        for k in range(7):
            gs_send(s, k).wait_send()

    def hidden(s, weights, slots):
        for k in range(4):
            x = rows[s, :, k * 1792 : (k + 1) * 1792]
            for i in range(2):
                v = jnp.dot(
                    x, weights[56 * i + 14 * k : 56 * i + 14 * k + 14].reshape(1792, 256), preferred_element_type=F32
                )
                acc[i] = v if k == 0 else acc[i] + v
            run(slots)
        g = acc[0]
        return g / (1.0 + jnp.exp(-g)) * acc[1]

    def copy_tag():
        tag = tgi[...].astype(F32)
        return jnp.concatenate([tag, tag], axis=1)

    PARTS = ((0, 0, TILES), (1, 0, 2), (1, 2, 2), (1, 4, 2), (1, 6, 1))

    def own_cols(p):
        return pl.ds(PARTS[p][1] * 128, PARTS[p][2] * 128)

    def block_cols(p, zi, core):
        return lanes((((z + zi) % 4) * 2 + core) * COLS + PARTS[p][1] * 128, PARTS[p][2] * 128)

    def sib_copy(p, zi):
        s = PARTS[p][0]
        return rcopy(
            part.at[s, :, block_cols(p, zi, 1 - c)], sibr.at[s, zi, :, own_cols(p)],
            s_ss.at[p, zi], s_rs.at[p, zi], sibling,
        )

    def partials(p, slots):
        s, first, count = PARTS[p]
        for zi in (2, 1, 3, 0):
            zz = (z + zi) % 4
            for q in range(first, first + count):
                at = pl.ds(112 + 2 * (q * 4 + zz), 2)
                v = jnp.dot(hid[s], hw[at].reshape(256, 256), preferred_element_type=F32)
                if s == 1:
                    v += jnp.dot(hid[2], hot[at].reshape(256, 256), preferred_element_type=F32)
                v = v.astype(BF)
                for core in range(2):
                    part[s, :, lanes((zz * 2 + core) * COLS + q * 128, 128)] = v[:, core * 128 : (core + 1) * 128]
            sib_copy(p, zi).start()
            run(slots)

    def pair_sum(p, zi):
        s = PARTS[p][0]
        return part[s, :, block_cols(p, zi, c)].astype(F32) + sibr[s, zi, :, own_cols(p)].astype(F32)

    DIRECT = (4,)

    lo_half, hi_half = pl.ds(0, HALF), pl.ds(HALF, HALF)

    def z_copy(p, k):
        s, cols = PARTS[p][0], own_cols(p)
        direct = p in DIRECT
        src, dst, direction = (
            (zs.at[s, 0, lo_half, cols], za.at[s, :, cols], 2 if direct else 1),
            (zs.at[s, 0, hi_half, cols], zb.at[s, :, cols], 2 if direct else -1),
            (zs.at[s, 1, hi_half, cols], rp.at[s, hi_half, cols], 1),
            (zs.at[s, 1, lo_half, cols], rp.at[s, lo_half, cols], 1),
            (zs.at[s, 2, lo_half, cols], rm.at[s, lo_half, cols], -1),
            (zs.at[s, 2, hi_half, cols], rm.at[s, hi_half, cols], -1),
        )[k]
        return rcopy(src, dst, z_ss.at[p, k], z_rs.at[p, k], z_dev(direction + 4))

    def reduce1(p):
        s, cols = PARTS[p][0], own_cols(p)
        sib_copy(p, 2).wait_recv()
        zs[s, 0, :, cols] = pair_sum(p, 2).astype(BF)
        z_copy(p, 0).start()
        z_copy(p, 1).start()
        sib_copy(p, 1).wait_recv()
        zs[s, 1, :, cols] = pair_sum(p, 1).astype(BF)
        z_copy(p, 2).start()
        if p in DIRECT:
            z_copy(p, 3).start()
        sib_copy(p, 3).wait_recv()
        zs[s, 2, :, cols] = pair_sum(p, 3).astype(BF)
        z_copy(p, 4).start()
        if p in DIRECT:
            z_copy(p, 5).start()

    def reduce2(p):
        s, cols = PARTS[p][0], own_cols(p)
        z_copy(p, 0).wait_recv()
        zs[s, 1, lo_half, cols] = (zs[s, 1, lo_half, cols].astype(F32) + za[s, :, cols].astype(F32)).astype(BF)
        z_copy(p, 3).start()
        z_copy(p, 1).wait_recv()
        zs[s, 2, hi_half, cols] = (zs[s, 2, hi_half, cols].astype(F32) + zb[s, :, cols].astype(F32)).astype(BF)
        z_copy(p, 5).start()

    def reduce3(p):
        s, cols = PARTS[p][0], own_cols(p)
        sib_copy(p, 0).wait_recv()
        for k in (2, 4, 3, 5):
            z_copy(p, k).wait_recv()
        total = pair_sum(p, 0) + rp[s, :, cols].astype(F32) + rm[s, :, cols].astype(F32)
        if p in DIRECT:
            for k in (0, 1):
                z_copy(p, k).wait_recv()
            total += jnp.concatenate([za[s, :, cols].astype(F32), zb[s, :, cols].astype(F32)], axis=0)
        eo[s, :, cols] = total.astype(BF)

    def reduce_drain(p):
        for zi in range(4):
            sib_copy(p, zi).wait_send()
        for k in range(6):
            z_copy(p, k).wait_send()

    def back_start(p):
        s, cols = PARTS[p][0], own_cols(p)

        def send(j, carry):
            peer = (e + j) % NE
            rcopy(
                eo.at[s, rows16(peer * CAP, CAP), cols], ret.at[rows16(s * SLOTS + e * CAP, CAP), cols],
                r_ss.at[p], r_rs.at[p], ep_dev(peer),
            ).start()
            return carry

        lax.fori_loop(1, NE, send, 0)
        ret[rows16(s * SLOTS + e * CAP, CAP), cols] = eo[s, rows16(e * CAP, CAP), cols]

    def back_wait(p):
        s, cols = PARTS[p][0], own_cols(p)
        n = (NE - 1) * CAP
        done = rcopy(
            eo.at[s, pl.ds(0, n), cols], ret.at[pl.ds(s * SLOTS, n), cols], r_ss.at[p], r_rs.at[p],
            ep_dev((e + 1) % NE),
        )
        done.wait_recv()
        done.wait_send()

    def final(p, j, at):
        peer = (w + j) % NW
        cols = own_cols(p)
        return rcopy(
            outb.at[rows16(peer * 16, 16), cols], fin.at[at, :, cols], f_ss.at[p - 1], f_rs.at[p - 1], wide_dev(peer)
        )

    def wait_bytes(ref, sem):
        pltpu.make_async_copy(ref, ref, sem).wait()

    def final_wait(p):
        wait_bytes(fin.at[pl.ds(0, NW - 1), :, own_cols(p)], f_rs.at[p - 1])

    def final_drain(p):
        wait_bytes(outb.at[pl.ds(0, (NW - 1) * 16), own_cols(p)], f_ss.at[p - 1])

    def combine(p):
        cols = own_cols(p)
        outb[:, cols] = jnp.dot(wc[...], ret[:, cols], preferred_element_type=F32).astype(BF)
        for j in range(1, NW):
            final(p, j, w).start()
        fin[w, :, cols] = outb[rows16(w * 16, 16), cols]

    run(5)
    wait_bytes(xin.at[pl.ds(0, NW - 1)], x_rs)
    wait_bytes(xmeta.at[pl.ds(0, NW - 1)], m_rs)
    make_plan()
    a2a_start(0)
    run_to(8 * CUT)
    a2a_wait(0)
    gather0(0)
    a2a_start(1)
    run_to(12 * CUT)
    gather1(0)
    a2a_wait(1)
    run_to(16 * CUT)
    gather2(0)
    gather0(1)
    run_to(19 * CUT)
    gather3(0)
    run_to(20 * CUT)
    gather4(0)
    hid[0] = hidden(0, hw, 1).astype(BF)
    gather1(1)
    partials(0, 1)
    gather2(1)
    reduce1(0)
    run_to(31 * CUT)
    gather3(1)
    run_to(32 * CUT)
    gather4(1)
    hid[1] = (hidden(1, hw, 1) * (1.0 - copy_tag())).astype(BF)
    reduce2(0)
    run_to(4 * LAG + FIRST)
    hid[2] = (hidden(1, hot, 1) * copy_tag()).astype(BF)
    reduce3(0)
    run_to(4 * LAG + FIRST + 4 * CUT)
    partials(1, 0)
    run(2)
    reduce1(1)
    run_to(4 * LAG + FIRST + 8 * CUT)
    partials(2, 0)
    reduce2(1)
    run(1)
    reduce1(2)
    run_to(T_SLOTS)
    back_start(0)
    run_to(4 * LAG + FIRST + 12 * CUT)
    partials(3, 0)
    reduce2(2)
    run(1)
    reduce1(3)
    run(T_STEPS)
    partials(4, 0)
    reduce3(1)
    back_start(1)
    reduce2(3)
    reduce1(4)
    reduce3(2)
    back_start(2)
    reduce3(3)
    back_start(3)
    reduce3(4)
    back_start(4)
    drain_slots()
    wait_bytes(xs.at[pl.ds(0, NW - 1)], x_ss)
    wait_bytes(xmeta.at[pl.ds(0, NW - 1)], m_ss)
    for s in range(STEPS):
        gather_drain(s)
    back_wait(0)
    back_wait(1)
    combine(1)
    back_wait(2)
    combine(2)
    back_wait(3)
    combine(3)
    back_wait(4)
    combine(4)
    for p in range(5):
        reduce_drain(p)

    def store(first, count):
        blocks = [fin[k, :, first * 128 : (first + count) * 128].astype(F32) for k in range(NW)]
        for q in range(count):
            line = jnp.concatenate([block[:, q * 128 : (q + 1) * 128] for block in blocks], axis=1)
            for s in range(STEPS):
                out[s, :, (first + q) * 1024 : (first + q + 1) * 1024] = line[s * 8 : (s + 1) * 8].astype(BF)

    for p in range(1, 5):
        final_wait(p)
        store(PARTS[p][1], PARTS[p][2])
    for p in range(1, 5):
        final_drain(p)


def shards(
    requests, routes, gates, replica, placement, copy_plan, capacity, gate_proj, up_proj, down_proj
):
    vmem = pl.BlockSpec(memory_space=pltpu.VMEM)
    smem = pl.BlockSpec(memory_space=pltpu.SMEM)
    hbm = pl.BlockSpec(memory_space=pl.ANY)
    dma = pltpu.SemaphoreType.DMA
    return pl.pallas_call(
        layer_kernel,
        out_shape=jax.ShapeDtypeStruct(requests.shape, BF),
        in_specs=[vmem, vmem, vmem, vmem, smem, smem, smem, hbm, hbm, hbm],
        out_specs=vmem,
        scratch_shapes=[
            pltpu.VMEM((NW, 16, COLS), BF),
            pltpu.VMEM((16, 128), F32),
            pltpu.VMEM((NW, 16, COLS), BF),
            pltpu.VMEM((NW, 16, 128), F32),
            pltpu.VMEM((STEPS, SLOTS, COLS), BF),
            pltpu.VMEM((SLOTS, 128), BF),
            pltpu.VMEM((SLOTS, 128), BF),
            pltpu.VMEM((STEPS, SLOTS, D), BF),
            pltpu.VMEM((168, 128, 256), BF),
            pltpu.VMEM((168, 128, 256), BF),
            pltpu.VMEM((4, RING, CHUNK, 256), BF),
            pltpu.VMEM((4, STAGE, CHUNK, 256), BF),
            pltpu.VMEM((len(MASKS), 16, 256), BF),
            pltpu.VMEM((2, SLOTS, HID), F32),
            pltpu.VMEM((3, SLOTS, HID), BF),
            pltpu.VMEM((STEPS, SLOTS, D), BF),
            pltpu.VMEM((STEPS, 4, SLOTS, COLS), BF),
            pltpu.VMEM((STEPS, 3, SLOTS, COLS), BF),
            pltpu.VMEM((STEPS, HALF, COLS), BF),
            pltpu.VMEM((STEPS, HALF, COLS), BF),
            pltpu.VMEM((STEPS, SLOTS, COLS), BF),
            pltpu.VMEM((STEPS, SLOTS, COLS), BF),
            pltpu.VMEM((STEPS, SLOTS, COLS), BF),
            pltpu.VMEM((STEPS * SLOTS, COLS), BF),
            pltpu.VMEM((128, STEPS * SLOTS), BF),
            pltpu.VMEM((128, COLS), BF),
            pltpu.VMEM((NW, 16, COLS), BF),
            dma,
            dma, dma, dma, dma,
            dma((2,)), dma((2,)), dma, dma,
            dma((4, STAGE)), dma((4, RING)),
            dma((2, 6)), dma((2, 6)), dma((2, 7)), dma((2, 7)),
            dma((5, 4)), dma((5, 4)), dma((5, 6)), dma((5, 6)),
            dma((5,)), dma((5,)), dma((4,)), dma((4,)),
        ],
        compiler_params=pltpu.CompilerParams(
            collective_id=0, has_side_effects=True, vmem_limit_bytes=62 * 1024 * 1024
        ),
        name="expert_layer",
    )(
        requests, jnp.swapaxes(routes, 1, 2), jnp.swapaxes(gates, 1, 2), replica.T, placement, copy_plan, capacity,
        gate_proj.reshape(TILES, NW, 128, HID), up_proj.reshape(TILES, NW, 128, HID), down_proj.reshape(HID, D),
    )


def solution(mesh):
    rows = P(None, ("ep", "wide"), None)
    placed = (
        rows, rows, rows, P(("ep", "wide"), None), P(), P(), P(),
        P("ep", None, "wide"), P("ep", None, "wide"), P("ep", "wide", None),
    )
    return jax.shard_map(shards, mesh=mesh, in_specs=placed, out_specs=rows, check_vma=False)
```

```python
import jax
import jax.numpy as jnp
from jax import lax
from jax.experimental import pallas as pl
from jax.experimental.pallas import tpu as pltpu
from jax.sharding import PartitionSpec as P

BF = jnp.bfloat16
F32 = jnp.float32
STEPS = 2
CAP = 16
NE = 16
NW = 8
GROUP = 64
D = 7168
COLS = D // NW
SLOTS = NE * CAP
HALF = SLOTS // 2
HID = 256

TILES = COLS // 128

STEP_XY = ((1, 0), (-1, 0), (0, 1), (0, -1))
TREES = (
    ((0, 0, 0), (1, 0, 2), (1, 0, 0), (1, 1, 2), (2, 0, 0), (2, 0, 3), (1, 2, 1), (2, 3, 0)),
    ((0, 0, 1), (3, 0, 1), (3, 0, 3), (2, 0, 2), (2, 0, 1), (3, 3, 3), (2, 1, 1), (3, 2, 0)),
    ((0, 0, 2), (0, 1, 1), (0, 1, 0), (0, 1, 2), (3, 1, 3), (1, 1, 3), (3, 1, 2), (3, 2, 2)),
    ((0, 0, 3), (0, 3, 3), (0, 3, 1), (0, 3, 0), (0, 2, 0), (3, 3, 2), (1, 3, 2), (1, 2, 3)),
)
LAG = 6
CUT = 2
CHUNK = 128 // CUT
CHUNKS = 42 * CUT
FIRST = 28 * CUT
T_SLOTS = CHUNKS + 3 * LAG
T_STEPS = CHUNKS + 4 * LAG
STAGE = LAG + 1
RING = 5 * LAG + 1


def relay_tables():
    relay, arrive = {}, [{} for _ in TREES]
    for tree, edges in enumerate(TREES):
        came = {(0, 0): (None, 0)}
        for x, y, link in edges:
            via, depth = came[(x, y)]
            to = ((x + STEP_XY[link][0]) % 4, (y + STEP_XY[link][1]) % 4)
            came[to] = (link, depth + 1)
            relay.setdefault((link, link ^ 1 if via is None else via), []).append(y * 4 + x)
            if to in OWNERS:
                arrive[tree].setdefault((link, LAG * depth), []).append(to[1] * 4 + to[0])
    return relay, arrive


OWNERS = ((1, 0), (1, 1), (3, 0), (3, 3), (0, 2))
RELAY, ARRIVE = relay_tables()
MASKS = [("relay", key) for key in sorted(RELAY)] + [
    ("arrive", tree, key) for tree in range(4) for key in sorted(ARRIVE[tree])
]
MASK_AT = {name: i for i, name in enumerate(MASKS)}


def rcopy(src, dst, ssem, rsem, dev):
    return pltpu.make_async_remote_copy(
        src_ref=src,
        dst_ref=dst,
        send_sem=ssem,
        recv_sem=rsem,
        device_id=dev,
        device_id_type=pl.DeviceIdType.MESH,
    )


def lanes(start, size):
    return pl.ds(pl.multiple_of(start, 128), size)


def rows16(start, size):
    return pl.ds(pl.multiple_of(start, 16), size)


def layer_kernel(
    req, routes, gates, replica, placement, copy_plan, capacity, gate, up, down, out,
    xs, meta, xin, xmeta, outg, tgo, tgi, rows, hw, hot, rb, sb, mk, acc, hid, part, sibr, zs, za, zb, rp, rm,
    eo, ret, wc, outb, fin,
    load_sem, x_ss, x_rs, m_ss, m_rs, a_ss, a_rs, t_ss, t_rs,
    b_ss, b_rs, gz_ss, gz_rs, gs_ss, gs_rs, s_ss, s_rs, z_ss, z_rs, r_ss, r_rs, f_ss, f_rs,
):
    e = lax.axis_index("ep")
    w = lax.axis_index("wide")
    ex, ey = e % 4, e // 4
    z, c = w // 2, w % 2

    def wide_dev(other):
        return {"ep": e, "wide": other}

    def ep_dev(other):
        return {"ep": other, "wide": w}

    def z_dev(shift):
        return wide_dev(((z + shift) % 4) * 2 + c)

    sibling = wide_dev(z * 2 + 1 - c)
    link_dev = [
        ep_dev(((ey + dy + 4) % 4) * 4 + (ex + dx + 4) % 4) for dx, dy in STEP_XY
    ]

    def load_weights(j, carry):
        for i, ref in enumerate((gate, up)):
            pltpu.make_async_copy(ref.at[:, j], hw.at[pl.ds(56 * i + TILES * j, TILES)], load_sem).start()
        return carry

    lax.fori_loop(0, NW, load_weights, 0)

    def load_down(j, carry):
        for half in range(2):
            pltpu.make_async_copy(
                down.at[pl.ds(half * 128, 128), lanes(j * 256, 256)], hw.at[112 + 2 * j + half], load_sem
            ).start()
        return carry

    lax.fori_loop(0, 28, load_down, 0)

    barrier = pltpu.get_barrier_semaphore()
    for j in range(1, NW):
        pl.semaphore_signal(barrier, inc=1, device_id=wide_dev((w + j) % NW), device_id_type=pl.DeviceIdType.MESH)
    for j in range(1, NE):
        pl.semaphore_signal(barrier, inc=1, device_id=ep_dev((e + j) % NE), device_id_type=pl.DeviceIdType.MESH)

    both = jnp.concatenate([req[0].astype(F32), req[1].astype(F32)], axis=0).astype(BF)
    for k in range(NW):
        for q in range(TILES):
            xs[k, :, q * 128 : (q + 1) * 128] = both[:, q * 1024 + k * 128 : q * 1024 + (k + 1) * 128]
    lane8 = lax.broadcasted_iota(jnp.int32, (8, 128), 1)
    for s in range(STEPS):
        line = jnp.zeros((8, 128), F32)
        for i, ref in enumerate((routes[s], replica[...], gates[s])):
            values = ref.astype(F32).T
            for k in range(2):
                line = jnp.where(lane8 == 2 * i + k, jnp.broadcast_to(values[:, k : k + 1], (8, 128)), line)
        meta[s * 8 : (s + 1) * 8, :] = line

    def spread_row(values):
        line = jnp.zeros((8, 128), jnp.int32)
        for i, value in enumerate(values):
            line = jnp.where(lane8 == i, value, line)
        return jnp.broadcast_to(line[0:1, :].astype(F32), (128, 128))

    home = placement[copy_plan[0]]
    place = ((ey - home // 4 + 4) % 4) * 4 + (ex - home % 4 + 4) % 4
    places = jnp.full((16, 256), place, jnp.int32)
    for i, name in enumerate(MASKS):
        mask = jnp.zeros((16, 256), F32)
        for at in RELAY[name[1]] if name[0] == "relay" else ARRIVE[name[1]][name[2]]:
            mask = jnp.where(places == at, 1.0, mask)
        mk[i] = mask.astype(BF)

    pl.semaphore_wait(barrier, NW - 1 + NE - 1)

    def exchange(j, peer, at):
        return (
            rcopy(xs.at[(w + j) % NW], xin.at[at], x_ss, x_rs, wide_dev(peer)),
            rcopy(meta, xmeta.at[at], m_ss, m_rs, wide_dev(peer)),
        )

    for j in range(1, NW):
        for copy in reversed(exchange(j, (w + j) % NW, w)):
            copy.start()
    xin[w] = xs[w]
    xmeta[w] = meta[...]
    pltpu.make_async_copy(hw, hw, load_sem).wait()

    def slot_copy(link, t):
        return rcopy(
            sb.at[link, t % STAGE], rb.at[link, t % RING], b_ss.at[link, t % STAGE], b_rs.at[link, t % RING],
            link_dev[link],
        )

    def chunk_of(ref, tree, n, later):
        block = n // CUT
        if later:
            block -= FIRST // CUT
            block = 112 + (block // 2 * 4 + tree) * 2 + block % 2
        else:
            block += tree * (FIRST // CUT)
        return ref.at[block, rows16(n % CUT * CHUNK, CHUNK)]

    def masked(block, mask):
        return block.reshape(CHUNK // 16, 16, 256) * mk[MASK_AT[mask]][None]

    def add(total, term):
        return term if total is None else total + term

    def step(t, own, own_later, recv, wait, send, deliver, deliver_later):
        if recv:
            for link in range(4):
                slot_copy(link, t - LAG).wait_recv()
        if send:
            for link in range(4):
                if wait:
                    slot_copy(link, t - STAGE).wait_send()
                total = None
                for k in range(4):
                    if (link, k) not in RELAY:
                        continue
                    if k == link ^ 1:
                        if own:
                            total = add(total, masked(chunk_of(hw, link, t, own_later)[...], ("relay", (link, k))))
                    elif recv:
                        total = add(total, masked(rb[k, (t - LAG) % RING], ("relay", (link, k))))
                sb[link, t % STAGE] = total.reshape(CHUNK, 256)
                slot_copy(link, t).start()
        if deliver:
            n = t - 4 * LAG
            for tree in range(4):
                total = None
                for link, behind in sorted(ARRIVE[tree]):
                    block = rb[link, (n + behind) % RING]
                    total = add(total, masked(block, ("arrive", tree, (link, behind))))
                chunk_of(hot, tree, n, deliver_later)[...] = total.reshape(CHUNK, 256)

    cursor = [0]

    def run_to(t1):
        t0 = cursor[0]
        t1 = max(t0, min(T_STEPS, t1))
        cursor[0] = t1
        marks = (LAG, STAGE, FIRST, CHUNKS, T_SLOTS, 4 * LAG, 4 * LAG + FIRST)
        cuts = sorted({t0, t1, *[x for x in marks if t0 < x < t1]})
        for lo, hi in zip(cuts[:-1], cuts[1:]):
            kind = (
                lo < CHUNKS, lo >= FIRST, lo >= LAG, lo >= STAGE, lo < T_SLOTS, lo >= 4 * LAG, lo >= 4 * LAG + FIRST
            )
            if hi - lo == 1:
                step(lo, *kind)
            else:
                def body(t, carry, kind=kind):
                    step(t, *kind)
                    return carry

                lax.fori_loop(lo, hi, body, 0)

    def run(count):
        run_to(cursor[0] + count * CUT)

    def drain_slots():
        def drain_send(t, carry):
            for link in range(4):
                slot_copy(link, t).wait_send()
            return carry

        lax.fori_loop(T_SLOTS - STAGE, T_SLOTS, drain_send, 0)

    def make_plan():
        picks = xmeta[...].reshape(128, 128)
        lane = lax.broadcasted_iota(jnp.int32, (128, 128), 1)
        line = lax.broadcasted_iota(jnp.int32, (128, 128), 0)
        lane_f = lane.astype(F32)
        second = (line // 8) % 2 == 1
        limits = jnp.where(
            second,
            spread_row([capacity[1, i] for i in range(NE)]),
            spread_row([capacity[0, i] for i in range(NE)]),
        )
        slot_of = spread_row([placement[i] for i in range(NE)])
        cand = spread_row([home] + [(home + copy_plan[i]) % NE for i in range(1, 4)])
        hot_id = jnp.full((128, 128), copy_plan[0], jnp.int32).astype(F32)
        zero = jnp.zeros((128, 128), F32)

        def spread(column):
            return jnp.broadcast_to(picks[:, column : column + 1], (128, 128))

        def total(v):
            return jnp.broadcast_to(jnp.sum(v, axis=1, keepdims=True), (128, 128))

        onehots, servers, copied = [], [], []
        for k in range(2):
            route, pick = spread(k), spread(2 + k)
            server = total(jnp.where(lane_f == route, slot_of, zero))
            chosen = total(jnp.where(lane_f == pick, cand, zero))
            is_hot = jnp.where(second, jnp.where(route == hot_id, 1.0, 0.0), 0.0)
            server = jnp.where(is_hot > 0.5, chosen, server)
            copied.append(jnp.where(pick > 0.5, is_hot, 0.0))
            servers.append(server)
            onehots.append(jnp.where(lane_f == server, 1.0, 0.0))
        earlier = jnp.where(lane < line, 1.0, 0.0) * jnp.where((line // 8) % 2 == (lane // 8) % 2, 1.0, 0.0)
        before = jnp.dot(earlier.astype(BF), (onehots[0] + onehots[1]).astype(BF), preferred_element_type=F32)
        lane_w = lax.broadcasted_iota(jnp.int32, (128, 512), 1).astype(F32)
        base = jnp.where(second, float(SLOTS), 0.0)
        matches = []
        for k in range(2):
            count = before if k == 0 else before + onehots[0]
            position = total(count * onehots[k])
            limit = total(limits * onehots[k])
            column = jnp.where(position < limit, base + servers[k] * CAP + position, -1.0)
            matches.append(jnp.where(lane_w == jnp.broadcast_to(column[:, :1], (128, 512)), 1.0, 0.0))

        def wide512(v):
            return jnp.broadcast_to(v[:, :1], (128, 512))

        wc[...] = (matches[0] * wide512(spread(4)) + matches[1] * wide512(spread(5))).astype(BF)
        dispatch = (matches[0] + matches[1]).astype(BF)
        tags = (matches[0] * wide512(copied[0]) + matches[1] * wide512(copied[1])).astype(BF)
        flat = xin[...].reshape(128, COLS)
        contract = (((0,), (0,)), ((), ()))
        for s in range(STEPS):
            outg[s] = lax.dot_general(
                dispatch[:, s * SLOTS : (s + 1) * SLOTS], flat, contract, preferred_element_type=F32
            ).astype(BF)
        tgo[...] = lax.dot_general(
            tags[:, SLOTS:], jnp.ones((128, 128), BF), contract, preferred_element_type=F32
        ).astype(BF)

    def a2a_start(s):
        def send(j, carry):
            peer = (e + j) % NE
            rcopy(
                outg.at[s, rows16(peer * CAP, CAP)], rows.at[s, rows16(e * CAP, CAP), lanes(w * COLS, COLS)],
                a_ss.at[s], a_rs.at[s], ep_dev(peer),
            ).start()
            if s == 1:
                rcopy(
                    tgo.at[rows16(peer * CAP, CAP)], tgi.at[rows16(e * CAP, CAP)], t_ss, t_rs, ep_dev(peer)
                ).start()
            return carry

        lax.fori_loop(1, NE, send, 0)
        rows[s, rows16(e * CAP, CAP), lanes(w * COLS, COLS)] = outg[s, rows16(e * CAP, CAP), :]
        if s == 1:
            tgi[rows16(e * CAP, CAP), :] = tgo[rows16(e * CAP, CAP), :]

    def a2a_wait(s):
        n = (NE - 1) * CAP
        done = rcopy(
            outg.at[s, pl.ds(0, n)], rows.at[s, pl.ds(0, n), lanes(w * COLS, COLS)], a_ss.at[s], a_rs.at[s],
            ep_dev((e + 1) % NE),
        )
        done.wait_recv()
        done.wait_send()
        if s == 1:
            done = rcopy(tgo.at[pl.ds(0, n)], tgi.at[pl.ds(0, n)], t_ss, t_rs, ep_dev((e + 1) % NE))
            done.wait_recv()
            done.wait_send()

    def shard(s, shift, core, half):
        col = (((z + shift + 4) % 4) * 2 + core) * COLS
        lo, n = (0, SLOTS) if half is None else (half * HALF, HALF)
        return rows.at[s, pl.ds(lo, n), lanes(col, COLS)]

    GZ = ((1, 0, 0), (1, 0, 1), (-1, 0, 1), (-1, 0, 0), (1, -1, 0), (-1, 1, 1))

    def gz_send(s, k):
        direction, shift, half = GZ[k]
        src = shard(s, shift, c, half)
        return rcopy(src, src, gz_ss.at[s, k], gz_rs.at[s, k], z_dev(direction + 4))

    def gz_wait(s, k):
        direction, shift, half = GZ[k]
        ref = shard(s, shift - direction, c, half)
        rcopy(ref, ref, gz_ss.at[s, k], gz_rs.at[s, k], z_dev(direction + 4)).wait_recv()

    GS = ((0, None), (-1, 0), (1, 1), (-1, 1), (1, 0), (2, 0), (2, 1))

    def gs_send(s, k):
        src = shard(s, GS[k][0], c, GS[k][1])
        return rcopy(src, src, gs_ss.at[s, k], gs_rs.at[s, k], sibling)

    def gs_wait(s, k):
        ref = shard(s, GS[k][0], 1 - c, GS[k][1])
        rcopy(ref, ref, gs_ss.at[s, k], gs_rs.at[s, k], sibling).wait_recv()

    def gather0(s):
        for k in (0, 2, 1, 3):
            gz_send(s, k).start()
        gs_send(s, 0).start()

    def gather1(s):
        gz_wait(s, 0)
        gz_send(s, 4).start()
        gs_send(s, 1).start()
        gz_wait(s, 2)
        gz_send(s, 5).start()
        gs_send(s, 2).start()

    def gather2(s):
        gz_wait(s, 1)
        gs_send(s, 3).start()
        gz_wait(s, 3)
        gs_send(s, 4).start()

    def gather3(s):
        gz_wait(s, 4)
        gs_send(s, 5).start()
        gz_wait(s, 5)
        gs_send(s, 6).start()

    def gather4(s):
        for k in range(7):
            gs_wait(s, k)

    def gather_drain(s):
        for k in range(6):
            gz_send(s, k).wait_send()
        for k in range(7):
            gs_send(s, k).wait_send()

    def hidden(s, weights, slots):
        for k in range(4):
            x = rows[s, :, k * 1792 : (k + 1) * 1792]
            for i in range(2):
                v = jnp.dot(
                    x, weights[56 * i + 14 * k : 56 * i + 14 * k + 14].reshape(1792, 256), preferred_element_type=F32
                )
                acc[i] = v if k == 0 else acc[i] + v
            run(slots)
        g = acc[0]
        return g / (1.0 + jnp.exp(-g)) * acc[1]

    def copy_tag():
        tag = tgi[...].astype(F32)
        return jnp.concatenate([tag, tag], axis=1)

    PARTS = ((0, 0, TILES), (1, 0, 2), (1, 2, 2), (1, 4, 2), (1, 6, 1))

    def own_cols(p):
        return pl.ds(PARTS[p][1] * 128, PARTS[p][2] * 128)

    def block_cols(p, zi, core):
        return lanes((((z + zi) % 4) * 2 + core) * COLS + PARTS[p][1] * 128, PARTS[p][2] * 128)

    def sib_copy(p, zi):
        s = PARTS[p][0]
        return rcopy(
            part.at[s, :, block_cols(p, zi, 1 - c)], sibr.at[s, zi, :, own_cols(p)],
            s_ss.at[p, zi], s_rs.at[p, zi], sibling,
        )

    def partials(p, slots):
        s, first, count = PARTS[p]
        for zi in (2, 1, 3, 0):
            zz = (z + zi) % 4
            for q in range(first, first + count):
                at = pl.ds(112 + 2 * (q * 4 + zz), 2)
                v = jnp.dot(hid[s], hw[at].reshape(256, 256), preferred_element_type=F32)
                if s == 1:
                    v += jnp.dot(hid[2], hot[at].reshape(256, 256), preferred_element_type=F32)
                v = v.astype(BF)
                for core in range(2):
                    part[s, :, lanes((zz * 2 + core) * COLS + q * 128, 128)] = v[:, core * 128 : (core + 1) * 128]
            sib_copy(p, zi).start()
            run(slots)

    def pair_sum(p, zi):
        s = PARTS[p][0]
        return part[s, :, block_cols(p, zi, c)].astype(F32) + sibr[s, zi, :, own_cols(p)].astype(F32)

    DIRECT = (4,)

    lo_half, hi_half = pl.ds(0, HALF), pl.ds(HALF, HALF)

    def z_copy(p, k):
        s, cols = PARTS[p][0], own_cols(p)
        direct = p in DIRECT
        src, dst, direction = (
            (zs.at[s, 0, lo_half, cols], za.at[s, :, cols], 2 if direct else 1),
            (zs.at[s, 0, hi_half, cols], zb.at[s, :, cols], 2 if direct else -1),
            (zs.at[s, 1, hi_half, cols], rp.at[s, hi_half, cols], 1),
            (zs.at[s, 1, lo_half, cols], rp.at[s, lo_half, cols], 1),
            (zs.at[s, 2, lo_half, cols], rm.at[s, lo_half, cols], -1),
            (zs.at[s, 2, hi_half, cols], rm.at[s, hi_half, cols], -1),
        )[k]
        return rcopy(src, dst, z_ss.at[p, k], z_rs.at[p, k], z_dev(direction + 4))

    def reduce1(p):
        s, cols = PARTS[p][0], own_cols(p)
        sib_copy(p, 2).wait_recv()
        zs[s, 0, :, cols] = pair_sum(p, 2).astype(BF)
        z_copy(p, 0).start()
        z_copy(p, 1).start()
        sib_copy(p, 1).wait_recv()
        zs[s, 1, :, cols] = pair_sum(p, 1).astype(BF)
        z_copy(p, 2).start()
        if p in DIRECT:
            z_copy(p, 3).start()
        sib_copy(p, 3).wait_recv()
        zs[s, 2, :, cols] = pair_sum(p, 3).astype(BF)
        z_copy(p, 4).start()
        if p in DIRECT:
            z_copy(p, 5).start()

    def reduce2(p):
        s, cols = PARTS[p][0], own_cols(p)
        z_copy(p, 0).wait_recv()
        zs[s, 1, lo_half, cols] = (zs[s, 1, lo_half, cols].astype(F32) + za[s, :, cols].astype(F32)).astype(BF)
        z_copy(p, 3).start()
        z_copy(p, 1).wait_recv()
        zs[s, 2, hi_half, cols] = (zs[s, 2, hi_half, cols].astype(F32) + zb[s, :, cols].astype(F32)).astype(BF)
        z_copy(p, 5).start()

    def reduce3(p):
        s, cols = PARTS[p][0], own_cols(p)
        sib_copy(p, 0).wait_recv()
        for k in (2, 4, 3, 5):
            z_copy(p, k).wait_recv()
        total = pair_sum(p, 0) + rp[s, :, cols].astype(F32) + rm[s, :, cols].astype(F32)
        if p in DIRECT:
            for k in (0, 1):
                z_copy(p, k).wait_recv()
            total += jnp.concatenate([za[s, :, cols].astype(F32), zb[s, :, cols].astype(F32)], axis=0)
        eo[s, :, cols] = total.astype(BF)

    def reduce_drain(p):
        for zi in range(4):
            sib_copy(p, zi).wait_send()
        for k in range(6):
            z_copy(p, k).wait_send()

    def back_start(p):
        s, cols = PARTS[p][0], own_cols(p)

        def send(j, carry):
            peer = (e + j) % NE
            rcopy(
                eo.at[s, rows16(peer * CAP, CAP), cols], ret.at[rows16(s * SLOTS + e * CAP, CAP), cols],
                r_ss.at[p], r_rs.at[p], ep_dev(peer),
            ).start()
            return carry

        lax.fori_loop(1, NE, send, 0)
        ret[rows16(s * SLOTS + e * CAP, CAP), cols] = eo[s, rows16(e * CAP, CAP), cols]

    def back_wait(p):
        s, cols = PARTS[p][0], own_cols(p)
        n = (NE - 1) * CAP
        done = rcopy(
            eo.at[s, pl.ds(0, n), cols], ret.at[pl.ds(s * SLOTS, n), cols], r_ss.at[p], r_rs.at[p],
            ep_dev((e + 1) % NE),
        )
        done.wait_recv()
        done.wait_send()

    def final(p, j, at):
        peer = (w + j) % NW
        cols = own_cols(p)
        return rcopy(
            outb.at[rows16(peer * 16, 16), cols], fin.at[at, :, cols], f_ss.at[p - 1], f_rs.at[p - 1], wide_dev(peer)
        )

    def wait_bytes(ref, sem):
        pltpu.make_async_copy(ref, ref, sem).wait()

    def final_wait(p):
        wait_bytes(fin.at[pl.ds(0, NW - 1), :, own_cols(p)], f_rs.at[p - 1])

    def final_drain(p):
        wait_bytes(outb.at[pl.ds(0, (NW - 1) * 16), own_cols(p)], f_ss.at[p - 1])

    def combine(p):
        cols = own_cols(p)
        outb[:, cols] = jnp.dot(wc[...], ret[:, cols], preferred_element_type=F32).astype(BF)
        for j in range(1, NW):
            final(p, j, w).start()
        fin[w, :, cols] = outb[rows16(w * 16, 16), cols]

    run(6)
    wait_bytes(xin.at[pl.ds(0, NW - 1)], x_rs)
    wait_bytes(xmeta.at[pl.ds(0, NW - 1)], m_rs)
    make_plan()
    a2a_start(0)
    run_to(9 * CUT)
    a2a_wait(0)
    gather0(0)
    a2a_start(1)
    run_to(13 * CUT)
    gather1(0)
    a2a_wait(1)
    run_to(16 * CUT)
    gather2(0)
    gather0(1)
    run_to(19 * CUT)
    gather3(0)
    run_to(20 * CUT)
    gather4(0)
    hid[0] = hidden(0, hw, 1).astype(BF)
    gather1(1)
    partials(0, 1)
    gather2(1)
    reduce1(0)
    run_to(31 * CUT)
    gather3(1)
    run_to(32 * CUT)
    gather4(1)
    hid[1] = (hidden(1, hw, 1) * (1.0 - copy_tag())).astype(BF)
    reduce2(0)
    run_to(4 * LAG + FIRST)
    hid[2] = (hidden(1, hot, 1) * copy_tag()).astype(BF)
    reduce3(0)
    run_to(4 * LAG + FIRST + 4 * CUT)
    partials(1, 0)
    run(2)
    reduce1(1)
    run_to(4 * LAG + FIRST + 8 * CUT)
    partials(2, 0)
    reduce2(1)
    run(1)
    reduce1(2)
    run_to(T_SLOTS)
    back_start(0)
    run_to(4 * LAG + FIRST + 12 * CUT)
    partials(3, 0)
    reduce2(2)
    run(1)
    reduce1(3)
    run(T_STEPS)
    partials(4, 0)
    reduce3(1)
    back_start(1)
    reduce2(3)
    reduce1(4)
    reduce3(2)
    back_start(2)
    reduce3(3)
    back_start(3)
    reduce3(4)
    back_start(4)
    back_wait(0)
    back_wait(1)
    combine(1)
    back_wait(2)
    combine(2)
    back_wait(3)
    combine(3)
    back_wait(4)
    combine(4)
    drain_slots()
    wait_bytes(xs.at[pl.ds(0, NW - 1)], x_ss)
    wait_bytes(xmeta.at[pl.ds(0, NW - 1)], m_ss)
    for s in range(STEPS):
        gather_drain(s)
    for p in range(5):
        reduce_drain(p)

    def store(first, count):
        blocks = [fin[k, :, first * 128 : (first + count) * 128].astype(F32) for k in range(NW)]
        for q in range(count):
            line = jnp.concatenate([block[:, q * 128 : (q + 1) * 128] for block in blocks], axis=1)
            for s in range(STEPS):
                out[s, :, (first + q) * 1024 : (first + q + 1) * 1024] = line[s * 8 : (s + 1) * 8].astype(BF)

    for p in range(1, 5):
        final_wait(p)
        store(PARTS[p][1], PARTS[p][2])
    for p in range(1, 5):
        final_drain(p)


def shards(
    requests, routes, gates, replica, placement, copy_plan, capacity, gate_proj, up_proj, down_proj
):
    vmem = pl.BlockSpec(memory_space=pltpu.VMEM)
    smem = pl.BlockSpec(memory_space=pltpu.SMEM)
    hbm = pl.BlockSpec(memory_space=pl.ANY)
    dma = pltpu.SemaphoreType.DMA
    return pl.pallas_call(
        layer_kernel,
        out_shape=jax.ShapeDtypeStruct(requests.shape, BF),
        in_specs=[vmem, vmem, vmem, vmem, smem, smem, smem, hbm, hbm, hbm],
        out_specs=vmem,
        scratch_shapes=[
            pltpu.VMEM((NW, 16, COLS), BF),
            pltpu.VMEM((16, 128), F32),
            pltpu.VMEM((NW, 16, COLS), BF),
            pltpu.VMEM((NW, 16, 128), F32),
            pltpu.VMEM((STEPS, SLOTS, COLS), BF),
            pltpu.VMEM((SLOTS, 128), BF),
            pltpu.VMEM((SLOTS, 128), BF),
            pltpu.VMEM((STEPS, SLOTS, D), BF),
            pltpu.VMEM((168, 128, 256), BF),
            pltpu.VMEM((168, 128, 256), BF),
            pltpu.VMEM((4, RING, CHUNK, 256), BF),
            pltpu.VMEM((4, STAGE, CHUNK, 256), BF),
            pltpu.VMEM((len(MASKS), 16, 256), BF),
            pltpu.VMEM((2, SLOTS, HID), F32),
            pltpu.VMEM((3, SLOTS, HID), BF),
            pltpu.VMEM((STEPS, SLOTS, D), BF),
            pltpu.VMEM((STEPS, 4, SLOTS, COLS), BF),
            pltpu.VMEM((STEPS, 3, SLOTS, COLS), BF),
            pltpu.VMEM((STEPS, HALF, COLS), BF),
            pltpu.VMEM((STEPS, HALF, COLS), BF),
            pltpu.VMEM((STEPS, SLOTS, COLS), BF),
            pltpu.VMEM((STEPS, SLOTS, COLS), BF),
            pltpu.VMEM((STEPS, SLOTS, COLS), BF),
            pltpu.VMEM((STEPS * SLOTS, COLS), BF),
            pltpu.VMEM((128, STEPS * SLOTS), BF),
            pltpu.VMEM((128, COLS), BF),
            pltpu.VMEM((NW, 16, COLS), BF),
            dma,
            dma, dma, dma, dma,
            dma((2,)), dma((2,)), dma, dma,
            dma((4, STAGE)), dma((4, RING)),
            dma((2, 6)), dma((2, 6)), dma((2, 7)), dma((2, 7)),
            dma((5, 4)), dma((5, 4)), dma((5, 6)), dma((5, 6)),
            dma((5,)), dma((5,)), dma((4,)), dma((4,)),
        ],
        compiler_params=pltpu.CompilerParams(
            collective_id=0, has_side_effects=True, vmem_limit_bytes=62 * 1024 * 1024
        ),
        name="expert_layer",
    )(
        requests, jnp.swapaxes(routes, 1, 2), jnp.swapaxes(gates, 1, 2), replica.T, placement, copy_plan, capacity,
        gate_proj.reshape(TILES, NW, 128, HID), up_proj.reshape(TILES, NW, 128, HID), down_proj.reshape(HID, D),
    )


def solution(mesh):
    rows = P(None, ("ep", "wide"), None)
    placed = (
        rows, rows, rows, P(("ep", "wide"), None), P(), P(), P(),
        P("ep", None, "wide"), P("ep", None, "wide"), P("ep", "wide", None),
    )
    return jax.shard_map(shards, mesh=mesh, in_specs=placed, out_specs=rows, check_vma=False)
```
